32 devices in a mesh: groups: 2 (over x), row: 8 (over z, y), col: 2 (over core).
Axes of the slice: x: 2, y: 2, z: 4, core: 2. Of those that a mesh axis runs over, the one named last changes fastest.
Arguments:
- cotangent: bfloat16 [32768, 1280], P(('row', 'col'), 'groups'), parts along dimension 1, may hold values from -6 to 6
- forward_input: bfloat16 [32768, 1280], P(('row', 'col'), 'groups'), parts along dimension 1, may hold values from -0.15625 to 0.15625
- basis_left: bfloat16 [32768, 64], P(('row', 'col')), may hold values from -0.1875 to 0.1875
- basis_right: bfloat16 [32768, 64], P(('row', 'col')), may hold values from -0.75 to 0.75
- coupling: bfloat16 [2048, 2, 1024], P('row', 'col'), may hold values from -0.125 to 0.125
- admissible: int32 [32, 2, 16], P('row', 'col'), may hold values 0 or 1
Outputs:
- adjoint: bfloat16 [32768, 1280], P(('row', 'col'), 'groups'), parts along dimension 1
- coupling_grad: bfloat16 [4096, 2, 1024], P(('groups', 'row'), 'col'), parts along dimension 0
The draws below stay inside these ranges and needn't reach their ends.
There are 2 independent parts, one for each index of `groups`. The reference program is written for one: setup_inputs(seed, part) draws one part's arguments, and reference() takes and returns one part's arrays. A program takes and returns all parts, laid end to end along the dimension named above; an argument that names none is the same for every part. Nothing has to cross between parts.
All inputs are finite; a program needn't handle non-finite values. No bound on the sum of `admissible` on one device may be relied on, other than what follows from the above.
Results may differ from the reference program's by a relative error of at most 0.0057.
Values may be sent and summed in bfloat16 or wider, within the bound.
No kernel may reach another device: no remote copies, remote signals or barrier semaphores. Data moves between devices by JAX's collectives and lax.ppermute only.
A program may use at most 128 MiB of HBM per device.

```python
import jax
import jax.numpy as jnp

CL = 1024
RANK = 64
CLUS_DEV = 2
CASES = 640
CLUSTERS = 32
ORDER = 32768
CORDER = 2048
HALF = 1024
N_ROW = 8


def touch_ends(result, rng, least, high):
    longest = result.shape.index(max(result.shape))
    spots = []
    for shift in (0, 1):
        where = [jax.random.randint(jax.random.fold_in(rng, axis), (), 0, length) for axis, length in enumerate(result.shape)]
        where[longest] = (where[longest] + shift) % result.shape[longest]
        spots.append(tuple(where))
    return result.at[spots[0]].set(least).at[spots[1]].set(high)


def block_levels(own_key, extent, cuts, smallest, high):
    def one(dim, blocks):
        heights = jax.random.uniform(jax.random.fold_in(jax.random.fold_in(own_key, 6), dim), (blocks,), jnp.float32, smallest / len(cuts), high / len(cuts))
        return jnp.repeat(jnp.exp(heights), extent[dim] // blocks).reshape((-1,) + (1,) * (len(extent) - dim - 1))

    factor_of = one(*cuts[0])
    for cut in cuts[1:]:
        factor_of = factor_of * one(*cut)
    return factor_of


def noise(own_key, extent, spread, bound, shards=(), held_as=jnp.bfloat16):
    drawn = jax.random.normal(own_key, extent, jnp.float32) * spread
    if len(shards) > 0:
        drawn = block_levels(own_key, extent, shards, -0.22, 0.18) * drawn
    return jnp.clip(drawn, min=-bound, max=bound).astype(held_as)


def setup_inputs(seed: int = 0, part: int = 0) -> dict:
    splits = jax.random.split(jax.random.key(seed), 7)
    part_keys = jax.random.split(jax.random.fold_in(splits[6], part), 7)
    return {
        "cotangent": noise(part_keys[0], (ORDER, CASES), 1.0, 6.0, ((0, 16),)),
        "forward_input": noise(part_keys[1], (ORDER, CASES), (0.25 * CASES ** -0.5), 0.15625, ((0, 16),)),
        "basis_left": noise(splits[2], (ORDER, RANK), CL ** -0.5, 0.1875, ((0, 16),)),
        "basis_right": noise(splits[3], (ORDER, RANK), RANK ** -0.5, 0.75, ((0, 16),)),
        "coupling": noise(splits[4], (CORDER, 2, HALF), CORDER ** -0.5, 0.125, ((0, 8), (1, 2))),
        "admissible": touch_ends((jax.random.randint(splits[5], (CLUSTERS, 2, CLUSTERS // 2), 0, 4) < 3).astype(jnp.int32), jax.random.fold_in(splits[5], 1), 0, 1),
    }


def reference(cotangent, forward_input, basis_left, basis_right, coupling, admissible):
    corder = CLUSTERS * RANK
    full = coupling.reshape(corder, 2, N_ROW, CLUS_DEV * RANK).transpose(0, 2, 1, 3).reshape(corder, corder)
    flags = admissible.reshape(CLUSTERS, 2, N_ROW, CLUS_DEV).transpose(0, 2, 1, 3).reshape(CLUSTERS, CLUSTERS)
    widened = jnp.repeat(jnp.repeat(flags.astype(jnp.float32), RANK, axis=0), RANK, axis=1)
    masked = (full.astype(jnp.float32) * widened).astype(jnp.bfloat16)
    left = basis_left.astype(jnp.float32).reshape(CLUSTERS, CL, RANK)
    right = basis_right.astype(jnp.float32).reshape(CLUSTERS, CL, RANK)
    projected = jnp.einsum("cnr,cnk->crk", left, cotangent.astype(jnp.float32).reshape(CLUSTERS, CL, CASES))
    projected = projected.reshape(corder, CASES).astype(jnp.bfloat16)
    coupled = jnp.dot(masked.T, projected, preferred_element_type=jnp.float32).astype(jnp.bfloat16)
    adjoint = jnp.einsum("cnr,crk->cnk", right, coupled.astype(jnp.float32).reshape(CLUSTERS, RANK, CASES))
    adjoint = adjoint.reshape(CLUSTERS * CL, CASES).astype(jnp.bfloat16)
    inputs = jnp.einsum("cnr,cnk->crk", right, forward_input.astype(jnp.float32).reshape(CLUSTERS, CL, CASES))
    inputs = inputs.reshape(corder, CASES).astype(jnp.bfloat16)
    grad = jnp.dot(projected, inputs.T, preferred_element_type=jnp.float32) * widened
    grad = grad.astype(jnp.bfloat16).reshape(corder, N_ROW, 2, CLUS_DEV * RANK).transpose(0, 2, 1, 3)
    return adjoint, grad.reshape(corder, 2, corder // 2)
```

```python
import functools

import jax
import jax.numpy as jnp
from jax import lax
from jax.experimental import pallas as pl
from jax.experimental.pallas import tpu as pltpu
from jax.sharding import PartitionSpec as P

CL = 1024
RANK = 64
CLUS_DEV = 2
BLK = CLUS_DEV * RANK
BF16 = jnp.bfloat16
F32 = jnp.float32

ENDS = (0, 3)
MIDS = (1, 2)
NN = (((1,), (0,)), ((), ()))
NT = (((1,), (1,)), ((), ()))
TN = (((0,), (0,)), ((), ()))


def along_z(pairs):
    return [(2 * a + y, 2 * b + y) for a, b in pairs for y in (0, 1)]


SWAP_OUTER = along_z([(0, 1), (1, 0), (2, 3), (3, 2)])
SWAP_INNER = along_z([(1, 2), (2, 1)])
OUTWARD = along_z([(1, 0), (2, 3)])
INWARD = along_z([(0, 1), (3, 2)])
SWAP_Y = [(r, r ^ 1) for r in range(8)]
SWAP_COL = [(0, 1), (1, 0)]


def dot(a, b, dims):
    return lax.dot_general(a, b, dims, preferred_element_type=F32)


def project(basis, x):
    out = jnp.einsum(
        "cnr,cnk->crk",
        basis.reshape(CLUS_DEV, CL, RANK),
        x.reshape(CLUS_DEV, CL, -1),
        preferred_element_type=F32,
    )
    return out.astype(BF16).reshape(BLK, -1)


def tile_mask(flags, a, p):
    rows = lax.broadcasted_iota(jnp.int32, (BLK, BLK), 0) < RANK
    cols = lax.broadcasted_iota(jnp.int32, (BLK, BLK), 1) < RANK
    f = [[flags[2 * a + i, 2 * p + j] for j in (0, 1)] for i in (0, 1)]
    return jnp.where(rows, jnp.where(cols, f[0][0], f[0][1]), jnp.where(cols, f[1][0], f[1][1])).astype(F32)


def mask_kernel(steps, at, flags, coupling, mine, send):
    z, y, h = at[0], at[1], at[2]
    for n, k in enumerate(steps):
        for out, side in ((mine, y), (send, 1 - y)):
            p = 2 * (z ^ k) + side
            for half in (0, 1):
                a = h if half == 0 else 1 - h
                tile = coupling[pl.ds(pl.multiple_of(a * BLK, BLK), BLK), pl.ds(pl.multiple_of(p * BLK, BLK), BLK)]
                tile = tile.astype(F32) * tile_mask(flags, a, p)
                out[n * BLK : (n + 1) * BLK, half * BLK : (half + 1) * BLK] = tile.T.astype(BF16)


def vmem(n):
    return [pl.BlockSpec(memory_space=pltpu.VMEM)] * n


def smem(n):
    return [pl.BlockSpec(memory_space=pltpu.SMEM)] * n


def mask(steps, at, flags, coupling):
    shape = jax.ShapeDtypeStruct((len(steps) * BLK, 2 * BLK), BF16)
    return pl.pallas_call(
        functools.partial(mask_kernel, steps),
        out_shape=(shape, shape),
        in_specs=smem(2) + vmem(1),
        out_specs=tuple(vmem(2)),
        name="mask",
    )(at, flags, coupling)


def local_sum(n, mine, part, blocks):
    rows = slice(n * BLK, (n + 1) * BLK)
    total = dot(mine[rows, :BLK], blocks[0][...], NN) + dot(mine[rows, BLK:], blocks[1][...], NN)
    return total + dot(part[rows, :BLK], blocks[2][...], NN) + dot(part[rows, BLK:], blocks[3][...], NN)


def partial_kernel(n, got, mine, part, *refs):
    total = local_sum(n, mine, part, refs[:4])
    for ref in refs[4 : 4 + got]:
        total = total + ref[...].astype(F32)
    refs[-1][...] = total.astype(BF16)


def partial(n, mine, part, blocks, got=()):
    cases = blocks[0].shape[1]
    return pl.pallas_call(
        functools.partial(partial_kernel, n, len(got)),
        out_shape=jax.ShapeDtypeStruct((BLK, cases), BF16),
        in_specs=vmem(6 + len(got)),
        out_specs=vmem(1)[0],
        name="partial",
    )(mine, part, *blocks, *got)


def adjoint_kernel(right, mine, part, b0, b1, b2, b3, f1, f2, out, coupled):
    step = pl.program_id(0)

    @pl.when(step == 0)
    def _():
        total = local_sum(1, mine, part, (b0, b1, b2, b3))
        total = total + f1[...].astype(F32) + f2[...].astype(F32)
        coupled[...] = total.astype(BF16)

    s = step // (pl.num_programs(0) // CLUS_DEV)
    c = coupled[pl.ds(pl.multiple_of(s * RANK, RANK), RANK), :]
    out[...] = dot(right[...], c, TN).astype(BF16)


def adjoint_of(right_t, mine, part, blocks, f1, f2):
    cases = blocks[0].shape[1]
    rows = 512
    whole = lambda x: pl.BlockSpec(x.shape, lambda i: (0, 0))
    rest = (mine, part, *blocks, f1, f2)
    return pl.pallas_call(
        adjoint_kernel,
        grid=(CLUS_DEV * CL // rows,),
        out_shape=jax.ShapeDtypeStruct((CLUS_DEV * CL, cases), BF16),
        in_specs=[pl.BlockSpec((RANK, rows), lambda i: (0, i))] + [whole(x) for x in rest],
        out_specs=pl.BlockSpec((rows, cases), lambda i: (i, 0)),
        scratch_shapes=[pltpu.VMEM((BLK, cases), BF16)],
        name="adjoint",
    )(right_t, *rest)


def back_kernel(pairs, *refs):
    b2, b3, out = refs[0], refs[1], refs[-1]
    for n in range(2):
        block = refs[2 + n * pairs][...]
        if pairs == 2:
            block = block + refs[3 + n * pairs][...]
        cols = slice(n * BLK, (n + 1) * BLK)
        out[:BLK, cols] = dot(b2[...], block, NT).astype(BF16)
        out[BLK:, cols] = dot(b3[...], block, NT).astype(BF16)


def back(pairs, b2, b3, inputs):
    return pl.pallas_call(
        functools.partial(back_kernel, pairs),
        out_shape=jax.ShapeDtypeStruct((2 * BLK, 2 * BLK), BF16),
        in_specs=vmem(2 + len(inputs)),
        out_specs=vmem(1)[0],
        name="back",
    )(b2, b3, *inputs)


def grad_kernel(at, flags, b0, b1, i0, i1, a2, o1, i2, o2, r1, r2, out):
    z, y, h = at[0], at[1], at[2]
    mid = ((z == 1) | (z == 2)).astype(jnp.int32)
    blocks = (i0[...], i1[...], a2[...] + o1[...], i2[...] + o2[...])
    owners = (z, z ^ 1, z ^ (2 + mid), z ^ (3 - mid))
    for n in range(4):
        for half, own in ((0, b0), (1, b1)):
            a = h if half == 0 else 1 - h
            rows = pl.ds(pl.multiple_of(a * BLK, BLK), BLK)
            p = 2 * owners[n] + y
            tile = dot(own[...], blocks[n], NT) * tile_mask(flags, a, p)
            out[rows, pl.ds(pl.multiple_of(p * BLK, BLK), BLK)] = tile.astype(BF16)
            p = 2 * owners[n] + 1 - y
            r = (r1, r2)[n // 2]
            tile = r[half * BLK : (half + 1) * BLK, (n % 2) * BLK : (n % 2 + 1) * BLK]
            tile = tile.astype(F32) * tile_mask(flags, a, p)
            out[rows, pl.ds(pl.multiple_of(p * BLK, BLK), BLK)] = tile.astype(BF16)


def grad_of(at, flags, *rest):
    return pl.pallas_call(
        grad_kernel,
        out_shape=jax.ShapeDtypeStruct((2 * BLK, 8 * BLK), BF16),
        in_specs=smem(2) + vmem(len(rest)),
        out_specs=vmem(1)[0],
        name="grad",
    )(at, flags, *rest)


def eight_rows(cotangent, forward_input, basis_left, basis_right, coupling, admissible):
    row, h = lax.axis_index("row"), lax.axis_index("col")
    at = jnp.stack([row // 2, row % 2, h]).astype(jnp.int32)
    flags = admissible[:, 0, :]
    coupling = coupling[:, 0, :]
    send = functools.partial(lax.ppermute, axis_name="row")
    swap = lambda x: lax.ppermute(x, "col", SWAP_COL)

    mine_far, out_far = mask((3, 2), at, flags, coupling)
    part_far = send(out_far, perm=SWAP_Y)
    own = project(basis_left, cotangent)
    pair = send(own, perm=SWAP_Y)
    other = swap(own)
    mine_near, out_near = mask((1, 0), at, flags, coupling)
    part_near = send(out_near, perm=SWAP_Y)
    inputs = project(basis_right, forward_input)
    a1 = send(inputs, perm=SWAP_OUTER)
    a2 = send(inputs, perm=SWAP_INNER)
    pair_other = swap(pair)
    blocks = (own, other, pair, pair_other)

    d1 = send(partial(0, mine_far, part_far, blocks), perm=INWARD)
    e1 = send(partial(1, mine_far, part_far, blocks), perm=INWARD)
    i2 = send(a1, perm=SWAP_INNER)
    o1 = send(a2, perm=OUTWARD)
    r1 = send(back(1, pair, pair_other, (inputs, a1)), perm=SWAP_Y)
    e2 = send(partial(1, mine_far, part_far, blocks, (d1,)), perm=SWAP_INNER)
    f2 = send(partial(0, mine_far, part_far, blocks, (e1,)), perm=SWAP_INNER)
    o2 = send(i2, perm=OUTWARD)
    f1 = send(partial(0, mine_near, part_near, blocks, (e2,)), perm=SWAP_OUTER)
    r2 = send(back(2, pair, pair_other, (a2, o1, i2, o2)), perm=SWAP_Y)
    grad = grad_of(at, flags, own, other, inputs, a1, a2, o1, i2, o2, r1, r2)
    adjoint = adjoint_of(basis_right.T, mine_near, part_near, blocks, f1, f2)
    return (adjoint, grad[:, None, :])


def any_rows(cotangent, forward_input, basis_left, basis_right, coupling, admissible):
    gathered = lax.all_gather(project(basis_left, cotangent), "col", axis=0, tiled=True)
    flags = admissible[:, 0, :].astype(BF16)
    widened = jnp.repeat(jnp.repeat(flags, RANK, axis=0), RANK, axis=1)
    masked = coupling[:, 0, :] * widened
    owned_columns = lax.all_to_all(masked, "row", split_axis=1, concat_axis=0, tiled=True)
    coupled = dot(owned_columns, lax.all_gather(gathered, "row", axis=0, tiled=True), TN).astype(BF16)
    adjoint = jnp.einsum(
        "cnr,crk->cnk",
        basis_right.reshape(CLUS_DEV, CL, RANK),
        coupled.reshape(CLUS_DEV, RANK, -1),
        preferred_element_type=F32,
    )
    adjoint = adjoint.astype(BF16).reshape(CLUS_DEV * CL, -1)
    inputs = project(basis_right, forward_input)
    outer = dot(gathered, lax.all_gather(inputs, "row", axis=0, tiled=True), NT)
    grad = (outer * widened.astype(F32)).astype(BF16)
    return (adjoint, grad[:, None, :])


def solution(mesh):
    return jax.shard_map(
        eight_rows if mesh.shape["row"] == 8 else any_rows,
        mesh=mesh,
        in_specs=(
            P(("row", "col"), "groups"),
            P(("row", "col"), "groups"),
            P(("row", "col"), None),
            P(("row", "col"), None),
            P("row", "col", None),
            P("row", "col", None),
        ),
        out_specs=(P(("row", "col"), "groups"), P(("groups", "row"), "col", None)),
        check_vma=False,
    )
```

```python
import functools

import jax
import jax.numpy as jnp
from jax import lax
from jax.experimental import pallas as pl
from jax.experimental.pallas import tpu as pltpu
from jax.sharding import PartitionSpec as P

CL = 1024
RANK = 64
CLUS_DEV = 2
BLK = CLUS_DEV * RANK
BF16 = jnp.bfloat16
F32 = jnp.float32

NN = (((1,), (0,)), ((), ()))
NT = (((1,), (1,)), ((), ()))
TN = (((0,), (0,)), ((), ()))
ROOM = 12 << 20
CHUNKS = 8


def dot(a, b, dims):
    return lax.dot_general(a, b, dims, preferred_element_type=F32)


def call(kernel, shapes, *args, near=(), name, **more):
    specs = [pl.BlockSpec(memory_space=m) for m in near]
    specs += [pl.BlockSpec(memory_space=pltpu.VMEM)] * (len(args) - len(near))
    held = [
        pltpu.with_memory_space_constraint(x, s.memory_space) if s.memory_space != pltpu.SMEM else x
        for s, x in zip(specs, args)
    ]
    more.setdefault("out_specs", tuple(pl.BlockSpec(memory_space=pltpu.VMEM) for _ in shapes))
    return pl.pallas_call(
        kernel,
        out_shape=tuple(shapes),
        in_specs=specs,
        name=name,
        compiler_params=pltpu.CompilerParams(vmem_limit_bytes=ROOM),
        **more,
    )(*held)


def place():
    row = lax.axis_index("row")
    return row // 2, row % 2, lax.axis_index("col")


def fetch_project_kernel(basis, x, out, basis_here, here, sems):
    rows = CLUS_DEV * CL // CHUNKS
    whole = pltpu.make_async_copy(basis, basis_here, sems.at[CHUNKS])
    whole.start()
    copies = []
    for i in range(CHUNKS):
        part = pl.ds(i * rows, rows)
        copies.append(pltpu.make_async_copy(x.at[part], here.at[part], sems.at[i]))
        copies[-1].start()
    whole.wait()
    for c in range(CLUS_DEV):
        total = None
        for i in range(c * CHUNKS // CLUS_DEV, (c + 1) * CHUNKS // CLUS_DEV):
            copies[i].wait()
            part = slice(i * rows, (i + 1) * rows)
            term = dot(basis_here[:, part], here[part], NN)
            total = term if total is None else total + term
        out[c * RANK : (c + 1) * RANK] = total.astype(BF16)


def fetch_project(basis_t, x):
    return call(
        fetch_project_kernel,
        [pltpu.VMEM((BLK, x.shape[1]), BF16)],
        basis_t,
        x,
        near=(pltpu.HBM, pltpu.HBM),
        scratch_shapes=[pltpu.VMEM(basis_t.shape, BF16), pltpu.VMEM(x.shape, BF16), pltpu.SemaphoreType.DMA((CHUNKS + 1,))],
        name="project",
    )[0]


def project_kernel(basis, x, out):
    for c in range(CLUS_DEV):
        part = slice(c * CL, (c + 1) * CL)
        out[c * RANK : (c + 1) * RANK] = dot(basis[:, part], x[part], NN).astype(BF16)


def project(basis_t, x):
    return call(project_kernel, [pltpu.VMEM((BLK, x.shape[1]), BF16)], basis_t, x, name="inputs")[0]


def tile_mask(flags, a, p):
    rows = lax.broadcasted_iota(jnp.int32, (BLK, BLK), 0) < RANK
    cols = lax.broadcasted_iota(jnp.int32, (BLK, BLK), 1) < RANK
    f = [[flags[2 * a + i, 2 * p + j] for j in (0, 1)] for i in (0, 1)]
    return jnp.where(rows, jnp.where(cols, f[0][0], f[0][1]), jnp.where(cols, f[1][0], f[1][1])).astype(F32)


def aligned(i):
    return pl.ds(pl.multiple_of(i * BLK, BLK), BLK)


def mask_kernel(steps, flags, coupling, mine, send):
    z, y, h = place()
    for n, k in enumerate(steps):
        for out, side in ((mine, y), (send, 1 - y)):
            p = 2 * (z ^ k) + side
            for half in (0, 1):
                a = h if half == 0 else 1 - h
                tile = coupling[aligned(a), aligned(p)].astype(F32) * tile_mask(flags, a, p)
                out[n * BLK : (n + 1) * BLK, half * BLK : (half + 1) * BLK] = tile.T.astype(BF16)


def mask(steps, flags, coupling):
    shape = pltpu.VMEM((len(steps) * BLK, 2 * BLK), BF16)
    return call(functools.partial(mask_kernel, steps), [shape] * 2, flags, coupling, near=(pltpu.SMEM,), name="mask")


def local_sum(n, mine, part, blocks):
    rows = slice(n * BLK, (n + 1) * BLK)
    total = dot(mine[rows, :BLK], blocks[0][...], NN) + dot(mine[rows, BLK:], blocks[1][...], NN)
    return total + dot(part[rows, :BLK], blocks[2][...], NN) + dot(part[rows, BLK:], blocks[3][...], NN)


def partial_kernel(n, got, mine, part, *refs):
    total = local_sum(n, mine, part, refs[:4])
    for ref in refs[4 : 4 + got]:
        total = total + ref[...].astype(F32)
    refs[-1][...] = total.astype(BF16)


def partial(n, mine, part, blocks, got=()):
    shape = pltpu.VMEM((BLK, blocks[0].shape[1]), BF16)
    return call(functools.partial(partial_kernel, n, len(got)), [shape], mine, part, *blocks, *got, name="partial")[0]


def adjoint_kernel(right, mine, part, b0, b1, b2, b3, f1, f2, out, coupled):
    step = pl.program_id(0)

    @pl.when(step == 0)
    def _():
        total = local_sum(1, mine, part, (b0, b1, b2, b3))
        total = total + f1[...].astype(F32) + f2[...].astype(F32)
        coupled[...] = total.astype(BF16)

    rows = out.shape[0]
    s = step // (CL // rows)
    c = coupled[pl.ds(pl.multiple_of(s * RANK, RANK), RANK), :]
    r = right[:, pl.ds(pl.multiple_of(step * rows, rows), rows)]
    out[...] = dot(r, c, TN).astype(BF16)


def adjoint_of(right_t, mine, part, blocks, f1, f2):
    cases = blocks[0].shape[1]
    rows = 256
    return call(
        adjoint_kernel,
        [jax.ShapeDtypeStruct((CLUS_DEV * CL, cases), BF16)],
        right_t,
        mine,
        part,
        *blocks,
        f1,
        f2,
        grid=(CLUS_DEV * CL // rows,),
        out_specs=(pl.BlockSpec((rows, cases), lambda i: (i, 0)),),
        scratch_shapes=[pltpu.VMEM((BLK, cases), BF16)],
        name="adjoint",
    )[0]


def back_kernel(b2, b3, *refs):
    out = refs[-1]
    for n, block in enumerate(refs[:-1]):
        cols = slice(n * BLK, (n + 1) * BLK)
        out[:BLK, cols] = dot(b2[...], block[...], NT).astype(BF16)
        out[BLK:, cols] = dot(b3[...], block[...], NT).astype(BF16)


def back(b2, b3, inputs):
    shape = pltpu.VMEM((2 * BLK, len(inputs) * BLK), BF16)
    return call(back_kernel, [shape], b2, b3, *inputs, name="back")[0]


def grad_kernel(flags, b0, b1, i0, i1, i2, i3, r1, r2, out):
    z, y, h = place()
    for n, block in enumerate((i0, i1, i2, i3)):
        for half, own in ((0, b0), (1, b1)):
            a = h if half == 0 else 1 - h
            p = 2 * (z ^ n) + y
            tile = dot(own[...], block[...], NT) * tile_mask(flags, a, p)
            out[aligned(a), aligned(p)] = tile.astype(BF16)
            p = 2 * (z ^ n) + 1 - y
            r = (r1, r2)[n // 2]
            tile = r[half * BLK : (half + 1) * BLK, (n % 2) * BLK : (n % 2 + 1) * BLK]
            tile = tile.astype(F32) * tile_mask(flags, a, p)
            out[aligned(a), aligned(p)] = tile.astype(BF16)


def grad_of(flags, *rest):
    shape = jax.ShapeDtypeStruct((2 * BLK, 8 * BLK), BF16)
    return call(grad_kernel, [shape], flags, *rest, near=(pltpu.SMEM,), name="grad")[0]


def swap_rows(x, bits):
    return lax.ppermute(x, "row", [(r, r ^ bits) for r in range(8)])


def swap_col(x):
    return lax.ppermute(x, "col", [(0, 1), (1, 0)])


def eight_rows(cotangent, forward_input, basis_left, basis_right, coupling, admissible):
    flags = admissible[:, 0, :]
    coupling = coupling[:, 0, :]
    right_t = basis_right.T

    own = fetch_project(basis_left.T, cotangent)
    pair = swap_rows(own, 1)
    other = swap_col(own)
    mine_far, out_far = mask((3, 2), flags, coupling)
    part_far = swap_rows(out_far, 1)
    inputs = project(right_t, forward_input)
    i1 = swap_rows(inputs, 2)
    i2 = swap_rows(inputs, 4)
    pair_other = swap_col(pair)
    blocks = (own, other, pair, pair_other)
    mine_near, out_near = mask((1, 0), flags, coupling)
    part_near = swap_rows(out_near, 1)

    s1 = swap_rows(partial(0, mine_far, part_far, blocks), 2)
    i3 = swap_rows(i2, 2)
    s2 = swap_rows(partial(1, mine_far, part_far, blocks, (s1,)), 4)
    s3 = swap_rows(partial(0, mine_near, part_near, blocks), 2)
    r1 = swap_rows(back(pair, pair_other, (inputs, i1)), 1)
    r2 = swap_rows(back(pair, pair_other, (i2, i3)), 1)
    grad = grad_of(flags, own, other, inputs, i1, i2, i3, r1, r2)
    adjoint = adjoint_of(right_t, mine_near, part_near, blocks, s2, s3)
    return (adjoint, grad[:, None, :])


def project_any(basis, x):
    out = jnp.einsum(
        "cnr,cnk->crk",
        basis.reshape(CLUS_DEV, CL, RANK),
        x.reshape(CLUS_DEV, CL, -1),
        preferred_element_type=F32,
    )
    return out.astype(BF16).reshape(BLK, -1)


def any_rows(cotangent, forward_input, basis_left, basis_right, coupling, admissible):
    gathered = lax.all_gather(project_any(basis_left, cotangent), "col", axis=0, tiled=True)
    flags = admissible[:, 0, :].astype(BF16)
    widened = jnp.repeat(jnp.repeat(flags, RANK, axis=0), RANK, axis=1)
    masked = coupling[:, 0, :] * widened
    owned_columns = lax.all_to_all(masked, "row", split_axis=1, concat_axis=0, tiled=True)
    coupled = dot(owned_columns, lax.all_gather(gathered, "row", axis=0, tiled=True), TN).astype(BF16)
    adjoint = jnp.einsum(
        "cnr,crk->cnk",
        basis_right.reshape(CLUS_DEV, CL, RANK),
        coupled.reshape(CLUS_DEV, RANK, -1),
        preferred_element_type=F32,
    )
    adjoint = adjoint.astype(BF16).reshape(CLUS_DEV * CL, -1)
    inputs = project_any(basis_right, forward_input)
    outer = dot(gathered, lax.all_gather(inputs, "row", axis=0, tiled=True), NT)
    grad = (outer * widened.astype(F32)).astype(BF16)
    return (adjoint, grad[:, None, :])


def solution(mesh):
    return jax.shard_map(
        eight_rows if mesh.shape["row"] == 8 else any_rows,
        mesh=mesh,
        in_specs=(
            P(("row", "col"), "groups"),
            P(("row", "col"), "groups"),
            P(("row", "col"), None),
            P(("row", "col"), None),
            P("row", "col", None),
            P("row", "col", None),
        ),
        out_specs=(P(("row", "col"), "groups"), P(("groups", "row"), "col", None)),
        check_vma=False,
    )
```

```python
import functools

import jax
import jax.numpy as jnp
from jax import lax
from jax.experimental import pallas as pl
from jax.experimental.pallas import tpu as pltpu
from jax.sharding import PartitionSpec as P

CL = 1024
RANK = 64
CLUS_DEV = 2
BLK = CLUS_DEV * RANK
BF16 = jnp.bfloat16
F32 = jnp.float32

NN = (((1,), (0,)), ((), ()))
NT = (((1,), (1,)), ((), ()))
TN = (((0,), (0,)), ((), ()))
ROOM = 12 << 20
CHUNKS = 8
PIECES = 8


def dot(a, b, dims):
    return lax.dot_general(a, b, dims, preferred_element_type=F32)


def call(kernel, shapes, *args, near=(), name, **more):
    specs = [pl.BlockSpec(memory_space=m) for m in near]
    specs += [pl.BlockSpec(memory_space=pltpu.VMEM)] * (len(args) - len(near))
    held = [
        pltpu.with_memory_space_constraint(x, s.memory_space) if s.memory_space != pltpu.SMEM else x
        for s, x in zip(specs, args)
    ]
    more.setdefault("out_specs", tuple(pl.BlockSpec(memory_space=pltpu.VMEM) for _ in shapes))
    return pl.pallas_call(
        kernel,
        out_shape=tuple(shapes),
        in_specs=specs,
        name=name,
        compiler_params=pltpu.CompilerParams(vmem_limit_bytes=ROOM),
        **more,
    )(*held)


def place():
    row = lax.axis_index("row")
    return row // 2, row % 2, lax.axis_index("col")


def aligned(i):
    return pl.ds(pl.multiple_of(i * BLK, BLK), BLK)


def tile_mask(flag, a, p):
    rows = lax.broadcasted_iota(jnp.int32, (BLK, BLK), 0) < RANK
    cols = lax.broadcasted_iota(jnp.int32, (BLK, BLK), 1) < RANK
    f = [[flag(2 * a + i, 2 * p + j) for j in (0, 1)] for i in (0, 1)]
    return jnp.where(rows, jnp.where(cols, f[0][0], f[0][1]), jnp.where(cols, f[1][0], f[1][1])).astype(F32)


def head_kernel(flags, coupling, left, right, cot, fin, own, inputs, mine_far, out_far, mine_near, out_near, *here):
    flags_s, coupling_s, left_s, right_s, cot_s, fin_s, sems = here
    rows = CLUS_DEV * CL // CHUNKS
    pairs = [(flags, flags_s), (coupling, coupling_s), (left, left_s)]
    pairs += [(cot.at[pl.ds(i * rows, rows)], cot_s.at[pl.ds(i * rows, rows)]) for i in range(CHUNKS)]
    pairs += [(right, right_s)]
    pairs += [(fin.at[pl.ds(i * rows, rows)], fin_s.at[pl.ds(i * rows, rows)]) for i in range(CHUNKS)]
    copies = [pltpu.make_async_copy(src, dst, sems.at[i]) for i, (src, dst) in enumerate(pairs)]
    for copy in copies:
        copy.start()

    z, y, h = place()
    copies[0].wait()
    copies[1].wait()
    for k in range(4):
        mine, out = (mine_far, out_far) if k > 1 else (mine_near, out_near)
        n = 1 - k % 2
        for ref, side in ((mine, y), (out, 1 - y)):
            p = 2 * (z ^ k) + side
            for half in (0, 1):
                a = h if half == 0 else 1 - h
                mask = tile_mask(lambda i, j: flags_s[i, 0, j], a, p)
                tile = coupling_s[aligned(a), aligned(p)].astype(F32) * mask
                ref[n * BLK : (n + 1) * BLK, half * BLK : (half + 1) * BLK] = tile.T.astype(BF16)

    at = 2
    for basis, x, result in ((left_s, cot_s, own), (right_s, fin_s, inputs)):
        copies[at].wait()
        for c in range(CLUS_DEV):
            total = None
            for i in range(c * CHUNKS // CLUS_DEV, (c + 1) * CHUNKS // CLUS_DEV):
                copies[at + 1 + i].wait()
                part = slice(i * rows, (i + 1) * rows)
                term = dot(basis[:, part], x[part], NN)
                total = term if total is None else total + term
            result[c * RANK : (c + 1) * RANK] = total.astype(BF16)
        at += CHUNKS + 1


def head(flags, coupling, left, right, cot, fin):
    block = pltpu.VMEM((BLK, cot.shape[1]), BF16)
    square = pltpu.VMEM((2 * BLK, 2 * BLK), BF16)
    args = (flags, coupling, left, right, cot, fin)
    return call(
        head_kernel,
        [block] * 2 + [square] * 4,
        *args,
        near=(pltpu.HBM,) * 6,
        scratch_shapes=[pltpu.SMEM(flags.shape, jnp.int32)]
        + [pltpu.VMEM(x.shape, BF16) for x in args[1:]]
        + [pltpu.SemaphoreType.DMA((4 + 2 * CHUNKS,))],
        name="head",
    )


def local_sum(n, mine, part, blocks):
    rows = slice(n * BLK, (n + 1) * BLK)
    total = dot(mine[rows, :BLK], blocks[0][...], NN) + dot(mine[rows, BLK:], blocks[1][...], NN)
    return total + dot(part[rows, :BLK], blocks[2][...], NN) + dot(part[rows, BLK:], blocks[3][...], NN)


def partial_kernel(n, got, mine, part, *refs):
    total = local_sum(n, mine, part, refs[:4])
    for ref in refs[4 : 4 + got]:
        total = total + ref[...].astype(F32)
    refs[-1][...] = total.astype(BF16)


def partial(n, mine, part, blocks, got=()):
    shape = pltpu.VMEM((BLK, blocks[0].shape[1]), BF16)
    return call(functools.partial(partial_kernel, n, len(got)), [shape], mine, part, *blocks, *got, name="partial")[0]


def adjoint_kernel(right, mine, part, b0, b1, b2, b3, f1, f2, out, made, sems):
    total = local_sum(1, mine, part, (b0, b1, b2, b3))
    total = total + f1[...].astype(F32) + f2[...].astype(F32)
    coupled = total.astype(BF16)
    rows = CLUS_DEV * CL // PIECES
    copies = []
    for i in range(PIECES):
        part = pl.ds(i * rows, rows)
        c = i * rows // CL
        made[part] = dot(right[:, i * rows : (i + 1) * rows], coupled[c * RANK : (c + 1) * RANK], TN).astype(BF16)
        copies.append(pltpu.make_async_copy(made.at[part], out.at[part], sems.at[i]))
        copies[-1].start()
    for copy in copies:
        copy.wait()


def adjoint_of(right_t, mine, part, blocks, f1, f2):
    shape = (CLUS_DEV * CL, blocks[0].shape[1])
    return call(
        adjoint_kernel,
        [pltpu.HBM(shape, BF16)],
        right_t,
        mine,
        part,
        *blocks,
        f1,
        f2,
        out_specs=(pl.BlockSpec(memory_space=pltpu.HBM),),
        scratch_shapes=[pltpu.VMEM(shape, BF16), pltpu.SemaphoreType.DMA((PIECES,))],
        name="adjoint",
    )[0]


def back_kernel(b2, b3, *refs):
    out = refs[-1]
    for n, block in enumerate(refs[:-1]):
        cols = slice(n * BLK, (n + 1) * BLK)
        out[:BLK, cols] = dot(b2[...], block[...], NT).astype(BF16)
        out[BLK:, cols] = dot(b3[...], block[...], NT).astype(BF16)


def back(b2, b3, inputs):
    shape = pltpu.VMEM((2 * BLK, len(inputs) * BLK), BF16)
    return call(back_kernel, [shape], b2, b3, *inputs, name="back")[0]


def grad_kernel(flags, b0, b1, i0, i1, i2, i3, r1, r2, out):
    z, y, h = place()
    for n, block in enumerate((i0, i1, i2, i3)):
        for half, own in ((0, b0), (1, b1)):
            a = h if half == 0 else 1 - h
            p = 2 * (z ^ n) + y
            tile = dot(own[...], block[...], NT) * tile_mask(lambda i, j: flags[i, j], a, p)
            out[aligned(a), aligned(p)] = tile.astype(BF16)
            p = 2 * (z ^ n) + 1 - y
            r = (r1, r2)[n // 2]
            tile = r[half * BLK : (half + 1) * BLK, (n % 2) * BLK : (n % 2 + 1) * BLK]
            tile = tile.astype(F32) * tile_mask(lambda i, j: flags[i, j], a, p)
            out[aligned(a), aligned(p)] = tile.astype(BF16)


def grad_of(flags, *rest):
    shape = jax.ShapeDtypeStruct((2 * BLK, 8 * BLK), BF16)
    return call(grad_kernel, [shape], flags, *rest, near=(pltpu.SMEM,), name="grad")[0]


def swap_rows(x, bits):
    return lax.ppermute(x, "row", [(r, r ^ bits) for r in range(8)])


def swap_col(x):
    return lax.ppermute(x, "col", [(0, 1), (1, 0)])


def eight_rows(cotangent, forward_input, basis_left, basis_right, coupling, admissible):
    flags = admissible[:, 0, :]
    coupling = coupling[:, 0, :]
    right_t = basis_right.T

    own, inputs, mine_far, out_far, mine_near, out_near = head(
        admissible, coupling, basis_left.T, right_t, cotangent, forward_input
    )
    pair = swap_rows(own, 1)
    other = swap_col(own)
    part_far = swap_rows(out_far, 1)
    i1 = swap_rows(inputs, 2)
    i2 = swap_rows(inputs, 4)
    pair, i1 = lax.optimization_barrier((pair, i1))
    pair_other = swap_col(pair)
    blocks = (own, other, pair, pair_other)
    part_near = swap_rows(out_near, 1)

    s1 = swap_rows(partial(0, mine_far, part_far, blocks), 2)
    i3 = swap_rows(i2, 2)
    s2 = swap_rows(partial(1, mine_far, part_far, blocks, (s1,)), 4)
    s3 = swap_rows(partial(0, mine_near, part_near, blocks), 2)
    r1 = swap_rows(back(pair, pair_other, (inputs, i1)), 1)
    r2 = swap_rows(back(pair, pair_other, (i2, i3)), 1)
    grad = grad_of(flags, own, other, inputs, i1, i2, i3, r1, r2)
    adjoint = adjoint_of(right_t, mine_near, part_near, blocks, s2, s3)
    return (adjoint, grad[:, None, :])


def project_any(basis, x):
    out = jnp.einsum(
        "cnr,cnk->crk",
        basis.reshape(CLUS_DEV, CL, RANK),
        x.reshape(CLUS_DEV, CL, -1),
        preferred_element_type=F32,
    )
    return out.astype(BF16).reshape(BLK, -1)


def any_rows(cotangent, forward_input, basis_left, basis_right, coupling, admissible):
    gathered = lax.all_gather(project_any(basis_left, cotangent), "col", axis=0, tiled=True)
    flags = admissible[:, 0, :].astype(BF16)
    widened = jnp.repeat(jnp.repeat(flags, RANK, axis=0), RANK, axis=1)
    masked = coupling[:, 0, :] * widened
    owned_columns = lax.all_to_all(masked, "row", split_axis=1, concat_axis=0, tiled=True)
    coupled = dot(owned_columns, lax.all_gather(gathered, "row", axis=0, tiled=True), TN).astype(BF16)
    adjoint = jnp.einsum(
        "cnr,crk->cnk",
        basis_right.reshape(CLUS_DEV, CL, RANK),
        coupled.reshape(CLUS_DEV, RANK, -1),
        preferred_element_type=F32,
    )
    adjoint = adjoint.astype(BF16).reshape(CLUS_DEV * CL, -1)
    inputs = project_any(basis_right, forward_input)
    outer = dot(gathered, lax.all_gather(inputs, "row", axis=0, tiled=True), NT)
    grad = (outer * widened.astype(F32)).astype(BF16)
    return (adjoint, grad[:, None, :])


def solution(mesh):
    return jax.shard_map(
        eight_rows if mesh.shape["row"] == 8 else any_rows,
        mesh=mesh,
        in_specs=(
            P(("row", "col"), "groups"),
            P(("row", "col"), "groups"),
            P(("row", "col"), None),
            P(("row", "col"), None),
            P("row", "col", None),
            P("row", "col", None),
        ),
        out_specs=(P(("row", "col"), "groups"), P(("groups", "row"), "col", None)),
        check_vma=False,
    )
```

```python
import functools

import jax
import jax.numpy as jnp
from jax import lax
from jax.experimental import pallas as pl
from jax.experimental.pallas import tpu as pltpu
from jax.sharding import PartitionSpec as P

CL = 1024
RANK = 64
CLUS_DEV = 2
BLK = CLUS_DEV * RANK
BF16 = jnp.bfloat16
F32 = jnp.float32

NN = (((1,), (0,)), ((), ()))
NT = (((1,), (1,)), ((), ()))
TN = (((0,), (0,)), ((), ()))
ROOM = 12 << 20
CHUNKS = 8
PIECES = 8


def dot(a, b, dims):
    return lax.dot_general(a, b, dims, preferred_element_type=F32)


def call(kernel, shapes, *args, near=(), name, **more):
    specs = [pl.BlockSpec(memory_space=m) for m in near]
    specs += [pl.BlockSpec(memory_space=pltpu.VMEM)] * (len(args) - len(near))
    held = [
        pltpu.with_memory_space_constraint(x, s.memory_space) if s.memory_space != pltpu.SMEM else x
        for s, x in zip(specs, args)
    ]
    more.setdefault("out_specs", tuple(pl.BlockSpec(memory_space=pltpu.VMEM) for _ in shapes))
    return pl.pallas_call(
        kernel,
        out_shape=tuple(shapes),
        in_specs=specs,
        name=name,
        compiler_params=pltpu.CompilerParams(vmem_limit_bytes=ROOM),
        **more,
    )(*held)


def place():
    row = lax.axis_index("row")
    return row // 2, row % 2, lax.axis_index("col")


def aligned(i):
    return pl.ds(pl.multiple_of(i * BLK, BLK), BLK)


def tile_mask(flag, a, p):
    rows = lax.broadcasted_iota(jnp.int32, (BLK, BLK), 0) < RANK
    cols = lax.broadcasted_iota(jnp.int32, (BLK, BLK), 1) < RANK
    f = [[flag(2 * a + i, 2 * p + j) for j in (0, 1)] for i in (0, 1)]
    return jnp.where(rows, jnp.where(cols, f[0][0], f[0][1]), jnp.where(cols, f[1][0], f[1][1])).astype(F32)


def masked_tile(flag, coupling, a, p):
    tile = coupling[aligned(a), aligned(p)] * tile_mask(flag, a, p).astype(BF16)
    return tile.T


def head_kernel(flags, coupling, left, right, cot, fin, own, packed, inputs, mine_far, mine, send, back_mask, *here):
    flags_s, coupling_s, left_s, right_s, cot_s, fin_s, sems = here
    rows = CLUS_DEV * CL // CHUNKS
    cases = cot.shape[1]
    pairs = [(flags, flags_s), (coupling, coupling_s), (left, left_s)]
    pairs += [(cot.at[pl.ds(i * rows, rows)], cot_s.at[pl.ds(i * rows, rows)]) for i in range(CHUNKS)]
    pairs += [(right, right_s)]
    pairs += [(fin.at[pl.ds(i * rows, rows)], fin_s.at[pl.ds(i * rows, rows)]) for i in range(CHUNKS)]
    copies = [pltpu.make_async_copy(src, dst, sems.at[i]) for i, (src, dst) in enumerate(pairs)]
    for copy in copies:
        copy.start()
    z, y, h = place()
    flag = lambda i, j: flags_s[i, 0, j]

    def project(at, basis, x, results):
        copies[at].wait()
        for c in range(CLUS_DEV):
            total = None
            for i in range(c * CHUNKS // CLUS_DEV, (c + 1) * CHUNKS // CLUS_DEV):
                copies[at + 1 + i].wait()
                part = slice(i * rows, (i + 1) * rows)
                term = dot(basis[:, part], x[part], NN)
                total = term if total is None else total + term
            for result in results:
                result[c * RANK : (c + 1) * RANK, :cases] = total.astype(BF16)

    copies[0].wait()
    copies[1].wait()
    for half in (0, 1):
        a = h if half == 0 else 1 - h
        for n in (0, 1):
            for ref, first, side in ((mine_far, 0, y), (packed, cases, 1 - y)):
                first += (2 * n + half) * BLK
                ref[:, first : first + BLK] = masked_tile(flag, coupling_s, a, 2 * (z ^ (3 - n)) + side)
    project(2, left_s, cot_s, (own, packed))
    for half in (0, 1):
        a = h if half == 0 else 1 - h
        cols = slice(half * BLK, (half + 1) * BLK)
        for k in (0, 1):
            at = slice(k * BLK, (k + 1) * BLK), cols
            mine[at] = masked_tile(flag, coupling_s, a, 2 * (z ^ k) + y)
            send[at] = masked_tile(flag, coupling_s, a, 2 * (z ^ k) + 1 - y)
        for k in range(4):
            back_mask[cols, k * BLK : (k + 1) * BLK] = tile_mask(flag, a, 2 * (z ^ k) + 1 - y).astype(BF16)
    project(3 + CHUNKS, right_s, fin_s, (inputs,))


def head(flags, coupling, left, right, cot, fin):
    cases = cot.shape[1]
    args = (flags, coupling, left, right, cot, fin)
    shapes = [(BLK, cases), (BLK, cases + 4 * BLK), (BLK, cases), (BLK, 4 * BLK)]
    shapes += [(2 * BLK, 2 * BLK)] * 2 + [(2 * BLK, 4 * BLK)]
    return call(
        head_kernel,
        [pltpu.VMEM(shape, BF16) for shape in shapes],
        *args,
        near=(pltpu.HBM,) * 6,
        scratch_shapes=[pltpu.SMEM(flags.shape, jnp.int32)]
        + [pltpu.VMEM(x.shape, BF16) for x in args[1:]]
        + [pltpu.SemaphoreType.DMA((4 + 2 * CHUNKS,))],
        name="head",
    )


def local_sum(mine, part, blocks):
    cases = blocks[0].shape[1]
    total = dot(mine[:, :BLK], blocks[0][...], NN) + dot(mine[:, BLK:], blocks[1][...], NN)
    return total + dot(part[:, :BLK], blocks[2][:, :cases], NN) + dot(part[:, BLK:], blocks[3][...], NN)


def far_kernel(n, mine, b0, b1, b2, b3, *refs):
    cols = slice(2 * n * BLK, 2 * (n + 1) * BLK)
    total = local_sum(mine[:, cols], b2[:, b0.shape[1] :][:, cols], (b0, b1, b2, b3))
    for ref in refs[:-1]:
        total = total + ref[...].astype(F32)
    refs[-1][...] = total.astype(BF16)


def far_sum(n, mine, blocks, *got):
    shape = pltpu.VMEM(blocks[0].shape, BF16)
    return call(functools.partial(far_kernel, n), [shape], mine, *blocks, *got, name="far")[0]


def near_sum_kernel(mine, part, b0, b1, b2, b3, out):
    out[...] = local_sum(mine[BLK:], part[BLK:], (b0, b1, b2, b3)).astype(BF16)


def near_sum(mine, part, blocks):
    return call(near_sum_kernel, [pltpu.VMEM(blocks[0].shape, BF16)], mine, part, *blocks, name="near")[0]


def adjoint_kernel(right, mine, part, b0, b1, b2, b3, s2, s3, out, made, sems):
    total = local_sum(mine[:BLK], part[:BLK], (b0, b1, b2, b3))
    total = total + s2[...].astype(F32) + s3[...].astype(F32)
    coupled = total.astype(BF16)
    rows = CLUS_DEV * CL // PIECES
    copies = []
    for i in range(PIECES):
        piece = pl.ds(i * rows, rows)
        c = i * rows // CL
        made[piece] = dot(right[:, i * rows : (i + 1) * rows], coupled[c * RANK : (c + 1) * RANK], TN).astype(BF16)
        copies.append(pltpu.make_async_copy(made.at[piece], out.at[piece], sems.at[i]))
        copies[-1].start()
    for copy in copies:
        copy.wait()


def adjoint_of(right_t, mine, part, blocks, s2, s3):
    shape = (CLUS_DEV * CL, s2.shape[1])
    return call(
        adjoint_kernel,
        [pltpu.HBM(shape, BF16)],
        right_t,
        mine,
        part,
        *blocks,
        s2,
        s3,
        out_specs=(pl.BlockSpec(memory_space=pltpu.HBM),),
        scratch_shapes=[pltpu.VMEM(shape, BF16), pltpu.SemaphoreType.DMA((PIECES,))],
        name="adjoint",
    )[0]


def tiles_kernel(after, b0, b1, *refs):
    out = refs[-1]
    for k, block in enumerate(refs[:-1]):
        cases = block.shape[1]
        cols = slice(k * BLK, (k + 1) * BLK)
        out[:BLK, cols] = dot(b0[:, :cases], block[...], NT).astype(BF16)
        out[BLK:, cols] = dot(b1[:, :cases], block[...], NT).astype(BF16)


def tiles(after, b0, b1, inputs, name):
    shape = pltpu.VMEM((2 * BLK, len(inputs) * BLK), BF16)
    return call(tiles_kernel, [shape], after, b0, b1, *inputs, name=name)[0]


def own_tiles_kernel(flags, *refs):
    z, y, h = place()
    tiles_kernel(*refs)
    out = refs[-1]
    for half in (0, 1):
        a = h if half == 0 else 1 - h
        for k in range(4):
            at = slice(half * BLK, (half + 1) * BLK), slice(k * BLK, (k + 1) * BLK)
            out[at] = out[at] * tile_mask(lambda i, j: flags[i, j], a, 2 * (z ^ k) + y).astype(BF16)


def own_tiles(flags, after, b0, b1, inputs):
    shape = pltpu.VMEM((2 * BLK, len(inputs) * BLK), BF16)
    return call(own_tiles_kernel, [shape], flags, after, b0, b1, *inputs, near=(pltpu.SMEM,), name="own_tiles")[0]


def grad_kernel(own, back, back_mask, out):
    z, y, h = place()
    for half in (0, 1):
        a = h if half == 0 else 1 - h
        for k in range(4):
            at = slice(half * BLK, (half + 1) * BLK), slice(k * BLK, (k + 1) * BLK)
            out[aligned(a), aligned(2 * (z ^ k) + y)] = own[at]
            out[aligned(a), aligned(2 * (z ^ k) + 1 - y)] = back[at] * back_mask[at]


def grad_of(own, back, back_mask):
    shape = jax.ShapeDtypeStruct((2 * BLK, 8 * BLK), BF16)
    return call(grad_kernel, [shape], own, back, back_mask, name="grad")[0]


def swap_rows(x, bits):
    return lax.ppermute(x, "row", [(r, r ^ bits) for r in range(8)])


def swap_col(x):
    return lax.ppermute(x, "col", [(0, 1), (1, 0)])


def swap_both(x):
    return lax.ppermute(x, ("row", "col"), [(d, d ^ 3) for d in range(16)])


def together(*arrays):
    return lax.optimization_barrier(arrays)


def eight_rows(cotangent, forward_input, basis_left, basis_right, coupling, admissible):
    flags = admissible[:, 0, :]
    right_t = basis_right.T

    own, packed, inputs, mine_far, mine, send, back_mask = head(
        admissible, coupling[:, 0, :], basis_left.T, right_t, cotangent, forward_input
    )
    pair = swap_rows(packed, 1)
    pair_other = swap_both(own)
    other = swap_col(own)
    i1 = swap_rows(inputs, 2)
    i2 = swap_rows(inputs, 4)
    blocks = (own, other, pair, pair_other)
    l3 = far_sum(0, mine_far, blocks)
    s1 = swap_rows(l3, 2)
    after = l3
    i3 = swap_rows(i2, 2)
    part = swap_rows(send, 1)
    l1 = near_sum(mine, part, blocks)
    s3 = swap_rows(l1, 2)
    l2 = far_sum(1, mine_far, blocks, s1)
    s2 = swap_rows(l2, 4)
    back = swap_rows(tiles(l3, pair, pair_other, (inputs, i1, i2, i3), "back"), 1)
    grad = grad_of(own_tiles(flags, after, own, other, (inputs, i1, i2, i3)), back, back_mask)
    adjoint = adjoint_of(right_t, mine, part, blocks, s2, s3)
    return (adjoint, grad[:, None, :])


def project_any(basis, x):
    out = jnp.einsum(
        "cnr,cnk->crk",
        basis.reshape(CLUS_DEV, CL, RANK),
        x.reshape(CLUS_DEV, CL, -1),
        preferred_element_type=F32,
    )
    return out.astype(BF16).reshape(BLK, -1)


def any_rows(cotangent, forward_input, basis_left, basis_right, coupling, admissible):
    gathered = lax.all_gather(project_any(basis_left, cotangent), "col", axis=0, tiled=True)
    flags = admissible[:, 0, :].astype(BF16)
    widened = jnp.repeat(jnp.repeat(flags, RANK, axis=0), RANK, axis=1)
    masked = coupling[:, 0, :] * widened
    owned_columns = lax.all_to_all(masked, "row", split_axis=1, concat_axis=0, tiled=True)
    coupled = dot(owned_columns, lax.all_gather(gathered, "row", axis=0, tiled=True), TN).astype(BF16)
    adjoint = jnp.einsum(
        "cnr,crk->cnk",
        basis_right.reshape(CLUS_DEV, CL, RANK),
        coupled.reshape(CLUS_DEV, RANK, -1),
        preferred_element_type=F32,
    )
    adjoint = adjoint.astype(BF16).reshape(CLUS_DEV * CL, -1)
    inputs = project_any(basis_right, forward_input)
    outer = dot(gathered, lax.all_gather(inputs, "row", axis=0, tiled=True), NT)
    grad = (outer * widened.astype(F32)).astype(BF16)
    return (adjoint, grad[:, None, :])


def solution(mesh):
    return jax.shard_map(
        eight_rows if mesh.shape["row"] == 8 else any_rows,
        mesh=mesh,
        in_specs=(
            P(("row", "col"), "groups"),
            P(("row", "col"), "groups"),
            P(("row", "col"), None),
            P(("row", "col"), None),
            P("row", "col", None),
            P("row", "col", None),
        ),
        out_specs=(P(("row", "col"), "groups"), P(("groups", "row"), "col", None)),
        check_vma=False,
    )
```

```python
import functools

import jax
import jax.numpy as jnp
from jax import lax
from jax.experimental import pallas as pl
from jax.experimental.pallas import tpu as pltpu
from jax.sharding import PartitionSpec as P

CL = 1024
RANK = 64
CLUS_DEV = 2
BLK = CLUS_DEV * RANK
BF16 = jnp.bfloat16
F32 = jnp.float32

NN = (((1,), (0,)), ((), ()))
NT = (((1,), (1,)), ((), ()))
TN = (((0,), (0,)), ((), ()))
ROOM = 12 << 20
COST = {'adjoint': 4, 'back': 0.3, 'own_tiles': 0.1, 'near': 0.3, 'far': 0.3, 'head': 3, 'grad': 0.3}
CHUNKS = 4
PIECES = 8


def dot(a, b, dims):
    return lax.dot_general(a, b, dims, preferred_element_type=F32)


def call(kernel, shapes, *args, near=(), name, **more):
    specs = [pl.BlockSpec(memory_space=m) for m in near]
    specs += [pl.BlockSpec(memory_space=pltpu.VMEM)] * (len(args) - len(near))
    held = [
        pltpu.with_memory_space_constraint(x, s.memory_space) if s.memory_space != pltpu.SMEM else x
        for s, x in zip(specs, args)
    ]
    more.setdefault("out_specs", tuple(pl.BlockSpec(memory_space=pltpu.VMEM) for _ in shapes))
    return pl.pallas_call(
        kernel,
        out_shape=tuple(shapes),
        in_specs=specs,
        name=name,
        compiler_params=pltpu.CompilerParams(vmem_limit_bytes=ROOM),
        cost_estimate=pl.CostEstimate(flops=int(COST.get(name, 1) * 1e9), bytes_accessed=0, transcendentals=0),
        **more,
    )(*held)


def place():
    row = lax.axis_index("row")
    return row // 2, row % 2, lax.axis_index("col")


def aligned(i):
    return pl.ds(pl.multiple_of(i * BLK, BLK), BLK)


def tile_mask(flag, a, p):
    rows = lax.broadcasted_iota(jnp.int32, (BLK, BLK), 0) < RANK
    cols = lax.broadcasted_iota(jnp.int32, (BLK, BLK), 1) < RANK
    f = [[flag(2 * a + i, 2 * p + j) for j in (0, 1)] for i in (0, 1)]
    return jnp.where(rows, jnp.where(cols, f[0][0], f[0][1]), jnp.where(cols, f[1][0], f[1][1])).astype(F32)


def masked_tile(flag, coupling, a, p):
    tile = coupling[aligned(a), aligned(p)] * tile_mask(flag, a, p).astype(BF16)
    return tile.T


def head_kernel(flags, coupling, left, right, cot, fin, own, packed, inputs, mine_far, mine, send, back_mask, *here):
    flags_s, coupling_s, left_s, right_s, cot_s, fin_s, sems = here
    rows = CLUS_DEV * CL // CHUNKS
    cases = cot.shape[1]
    pairs = [(flags, flags_s), (coupling, coupling_s), (left, left_s)]
    pairs += [(cot.at[pl.ds(i * rows, rows)], cot_s.at[pl.ds(i * rows, rows)]) for i in range(CHUNKS)]
    pairs += [(right, right_s)]
    pairs += [(fin.at[pl.ds(i * rows, rows)], fin_s.at[pl.ds(i * rows, rows)]) for i in range(CHUNKS)]
    copies = [pltpu.make_async_copy(src, dst, sems.at[i]) for i, (src, dst) in enumerate(pairs)]
    for copy in copies:
        copy.start()
    z, y, h = place()
    flag = lambda i, j: flags_s[i, 0, j]

    def project(at, basis, x, results):
        copies[at].wait()
        for c in range(CLUS_DEV):
            total = None
            for i in range(c * CHUNKS // CLUS_DEV, (c + 1) * CHUNKS // CLUS_DEV):
                copies[at + 1 + i].wait()
                part = slice(i * rows, (i + 1) * rows)
                term = dot(basis[:, part], x[part], NN)
                total = term if total is None else total + term
            for result in results:
                result[c * RANK : (c + 1) * RANK, :cases] = total.astype(BF16)

    copies[0].wait()
    copies[1].wait()
    for half in (0, 1):
        a = h if half == 0 else 1 - h
        for n in (0, 1):
            for ref, first, side in ((mine_far, 0, y), (packed, cases, 1 - y)):
                first += (2 * n + half) * BLK
                ref[:, first : first + BLK] = masked_tile(flag, coupling_s, a, 2 * (z ^ (3 - n)) + side)
    project(2, left_s, cot_s, (own, packed))
    for half in (0, 1):
        a = h if half == 0 else 1 - h
        cols = slice(half * BLK, (half + 1) * BLK)
        for k in (0, 1):
            at = slice(k * BLK, (k + 1) * BLK), cols
            mine[at] = masked_tile(flag, coupling_s, a, 2 * (z ^ k) + y)
            send[at] = masked_tile(flag, coupling_s, a, 2 * (z ^ k) + 1 - y)
        for k in range(4):
            back_mask[cols, k * BLK : (k + 1) * BLK] = tile_mask(flag, a, 2 * (z ^ k) + 1 - y).astype(BF16)
    project(3 + CHUNKS, right_s, fin_s, (inputs,))


def head(flags, coupling, left, right, cot, fin):
    cases = cot.shape[1]
    args = (flags, coupling, left, right, cot, fin)
    shapes = [(BLK, cases), (BLK, cases + 4 * BLK), (BLK, cases), (BLK, 4 * BLK)]
    shapes += [(2 * BLK, 2 * BLK)] * 2 + [(2 * BLK, 4 * BLK)]
    return call(
        head_kernel,
        [pltpu.VMEM(shape, BF16) for shape in shapes],
        *args,
        near=(pltpu.HBM,) * 6,
        scratch_shapes=[pltpu.SMEM(flags.shape, jnp.int32)]
        + [pltpu.VMEM(x.shape, BF16) for x in args[1:]]
        + [pltpu.SemaphoreType.DMA((4 + 2 * CHUNKS,))],
        name="head",
    )


def local_sum(mine, part, blocks):
    cases = blocks[0].shape[1]
    total = dot(mine[:, :BLK], blocks[0][...], NN) + dot(mine[:, BLK:], blocks[1][...], NN)
    return total + dot(part[:, :BLK], blocks[2][:, :cases], NN) + dot(part[:, BLK:], blocks[3][...], NN)


def far_kernel(n, got, mine, b0, b1, b2, b3, *refs):
    cols = slice(2 * n * BLK, 2 * (n + 1) * BLK)
    total = local_sum(mine[:, cols], b2[:, b0.shape[1] :][:, cols], (b0, b1, b2, b3))
    for ref in refs[:got]:
        total = total + ref[...].astype(F32)
    refs[-1][...] = total.astype(BF16)


def far_sum(n, mine, blocks, got=(), after=()):
    shape = pltpu.VMEM(blocks[0].shape, BF16)
    return call(functools.partial(far_kernel, n, len(got)), [shape], mine, *blocks, *got, *after, name="far")[0]


def near_sum_kernel(mine, part, b0, b1, b2, b3, *refs):
    out = refs[-1]
    out[...] = local_sum(mine[BLK:], part[BLK:], (b0, b1, b2, b3)).astype(BF16)


def near_sum(mine, part, blocks, after=()):
    return call(near_sum_kernel, [pltpu.VMEM(blocks[0].shape, BF16)], mine, part, *blocks, *after, name="near")[0]


def adjoint_kernel(right, mine, part, b0, b1, b2, b3, s2, s3, out, done, made, sems):
    total = local_sum(mine[:BLK], part[:BLK], (b0, b1, b2, b3))
    total = total + s2[...].astype(F32) + s3[...].astype(F32)
    coupled = total.astype(BF16)
    rows = CLUS_DEV * CL // PIECES
    copies = []
    for i in range(PIECES):
        piece = pl.ds(i * rows, rows)
        c = i * rows // CL
        made[piece] = dot(right[:, i * rows : (i + 1) * rows], coupled[c * RANK : (c + 1) * RANK], TN).astype(BF16)
        copies.append(pltpu.make_async_copy(made.at[piece], out.at[piece], sems.at[i]))
        copies[-1].start()
    for copy in copies:
        copy.wait()
    done[...] = jnp.zeros_like(done)


def adjoint_of(right_t, mine, part, blocks, s2, s3):
    shape = (CLUS_DEV * CL, s2.shape[1])
    return call(
        adjoint_kernel,
        [pltpu.HBM(shape, BF16), pltpu.VMEM((16, BLK), BF16)],
        right_t,
        mine,
        part,
        *blocks,
        s2,
        s3,
        out_specs=(pl.BlockSpec(memory_space=pltpu.HBM), pl.BlockSpec(memory_space=pltpu.VMEM)),
        scratch_shapes=[pltpu.VMEM(shape, BF16), pltpu.SemaphoreType.DMA((PIECES,))],
        name="adjoint",
    )


def tiles_kernel(after, b0, b1, *refs):
    out = refs[-1]
    for k, block in enumerate(refs[:-1]):
        cases = block.shape[1]
        cols = slice(k * BLK, (k + 1) * BLK)
        out[:BLK, cols] = dot(b0[:, :cases], block[...], NT).astype(BF16)
        out[BLK:, cols] = dot(b1[:, :cases], block[...], NT).astype(BF16)


def tiles(after, b0, b1, inputs, name):
    shape = pltpu.VMEM((2 * BLK, len(inputs) * BLK), BF16)
    return call(tiles_kernel, [shape], after, b0, b1, *inputs, name=name)[0]


def own_tiles_kernel(flags, *refs):
    z, y, h = place()
    tiles_kernel(*refs)
    out = refs[-1]
    for half in (0, 1):
        a = h if half == 0 else 1 - h
        for k in range(4):
            at = slice(half * BLK, (half + 1) * BLK), slice(k * BLK, (k + 1) * BLK)
            out[at] = out[at] * tile_mask(lambda i, j: flags[i, j], a, 2 * (z ^ k) + y).astype(BF16)


def own_tiles(flags, after, b0, b1, inputs):
    shape = pltpu.VMEM((2 * BLK, len(inputs) * BLK), BF16)
    return call(own_tiles_kernel, [shape], flags, after, b0, b1, *inputs, near=(pltpu.SMEM,), name="own_tiles")[0]


def grad_kernel(after, own, back, back_mask, out):
    z, y, h = place()
    for half in (0, 1):
        a = h if half == 0 else 1 - h
        for k in range(4):
            at = slice(half * BLK, (half + 1) * BLK), slice(k * BLK, (k + 1) * BLK)
            out[aligned(a), aligned(2 * (z ^ k) + y)] = own[at]
            out[aligned(a), aligned(2 * (z ^ k) + 1 - y)] = back[at] * back_mask[at]


def grad_of(after, own, back, back_mask):
    shape = jax.ShapeDtypeStruct((2 * BLK, 8 * BLK), BF16)
    return call(grad_kernel, [shape], after, own, back, back_mask, name="grad")[0]


def swap_rows(x, bits):
    return lax.ppermute(x, "row", [(r, r ^ bits) for r in range(8)])


def swap_col(x):
    return lax.ppermute(x, "col", [(0, 1), (1, 0)])


def swap_both(x):
    return lax.ppermute(x, ("row", "col"), [(d, d ^ 3) for d in range(16)])


def together(*arrays):
    return lax.optimization_barrier(arrays)


def eight_rows(cotangent, forward_input, basis_left, basis_right, coupling, admissible):
    flags = admissible[:, 0, :]
    right_t = basis_right.T

    own, packed, inputs, mine_far, mine, send, back_mask = head(
        admissible, coupling[:, 0, :], basis_left.T, right_t, cotangent, forward_input
    )
    pair = swap_rows(packed, 1)
    pair_other = swap_both(own)
    other = swap_col(own)
    i1 = swap_rows(inputs, 2)
    i2 = swap_rows(inputs, 4)
    blocks = (own, other, pair, pair_other)
    l3 = far_sum(0, mine_far, blocks, (), (i1, i2))
    s1 = swap_rows(l3, 2)
    i3 = swap_rows(i2, 2)
    part = swap_rows(send, 1)
    l2 = far_sum(1, mine_far, blocks, (s1,))
    s2 = swap_rows(l2, 4)
    l1 = near_sum(mine, part, blocks)
    s3 = swap_rows(l1, 2)
    back = swap_rows(tiles(l3, pair, pair_other, (inputs, i1, i2, i3), "back"), 1)
    tiles_here = own_tiles(flags, l3, own, other, (inputs, i1, i2, i3))
    adjoint, done = adjoint_of(right_t, mine, part, blocks, s2, s3)
    grad = grad_of(done, tiles_here, back, back_mask)
    return (adjoint, grad[:, None, :])


def project_any(basis, x):
    out = jnp.einsum(
        "cnr,cnk->crk",
        basis.reshape(CLUS_DEV, CL, RANK),
        x.reshape(CLUS_DEV, CL, -1),
        preferred_element_type=F32,
    )
    return out.astype(BF16).reshape(BLK, -1)


def any_rows(cotangent, forward_input, basis_left, basis_right, coupling, admissible):
    gathered = lax.all_gather(project_any(basis_left, cotangent), "col", axis=0, tiled=True)
    flags = admissible[:, 0, :].astype(BF16)
    widened = jnp.repeat(jnp.repeat(flags, RANK, axis=0), RANK, axis=1)
    masked = coupling[:, 0, :] * widened
    owned_columns = lax.all_to_all(masked, "row", split_axis=1, concat_axis=0, tiled=True)
    coupled = dot(owned_columns, lax.all_gather(gathered, "row", axis=0, tiled=True), TN).astype(BF16)
    adjoint = jnp.einsum(
        "cnr,crk->cnk",
        basis_right.reshape(CLUS_DEV, CL, RANK),
        coupled.reshape(CLUS_DEV, RANK, -1),
        preferred_element_type=F32,
    )
    adjoint = adjoint.astype(BF16).reshape(CLUS_DEV * CL, -1)
    inputs = project_any(basis_right, forward_input)
    outer = dot(gathered, lax.all_gather(inputs, "row", axis=0, tiled=True), NT)
    grad = (outer * widened.astype(F32)).astype(BF16)
    return (adjoint, grad[:, None, :])


def solution(mesh):
    return jax.shard_map(
        eight_rows if mesh.shape["row"] == 8 else any_rows,
        mesh=mesh,
        in_specs=(
            P(("row", "col"), "groups"),
            P(("row", "col"), "groups"),
            P(("row", "col"), None),
            P(("row", "col"), None),
            P("row", "col", None),
            P("row", "col", None),
        ),
        out_specs=(P(("row", "col"), "groups"), P(("groups", "row"), "col", None)),
        check_vma=False,
    )
```

```python
import functools

import jax
import jax.numpy as jnp
from jax import lax
from jax.experimental import pallas as pl
from jax.experimental.pallas import tpu as pltpu
from jax.sharding import PartitionSpec as P

CL = 1024
RANK = 64
CLUS_DEV = 2
BLK = CLUS_DEV * RANK
BF16 = jnp.bfloat16
F32 = jnp.float32

NN = (((1,), (0,)), ((), ()))
NT = (((1,), (1,)), ((), ()))
TN = (((0,), (0,)), ((), ()))
ROOM = 12 << 20
COST = {'head': 3, 'near': 0.3, 'far': 0.3, 'back': 0.3, 'back3': 0.3, 'back1': 0.3, 'own_tiles': 0.1, 'results': 4}
CHUNKS = 4
PIECES = 8


def dot(a, b, dims):
    return lax.dot_general(a, b, dims, preferred_element_type=F32)


def call(kernel, shapes, *args, near=(), name, **more):
    specs = [pl.BlockSpec(memory_space=m) for m in near]
    specs += [pl.BlockSpec(memory_space=pltpu.VMEM)] * (len(args) - len(near))
    held = [
        pltpu.with_memory_space_constraint(x, s.memory_space) if s.memory_space != pltpu.SMEM else x
        for s, x in zip(specs, args)
    ]
    more.setdefault("out_specs", tuple(pl.BlockSpec(memory_space=pltpu.VMEM) for _ in shapes))
    return pl.pallas_call(
        kernel,
        out_shape=tuple(shapes),
        in_specs=specs,
        name=name,
        compiler_params=pltpu.CompilerParams(vmem_limit_bytes=ROOM),
        cost_estimate=pl.CostEstimate(flops=int(COST.get(name, 1) * 1e9), bytes_accessed=0, transcendentals=0),
        **more,
    )(*held)


def place():
    row = lax.axis_index("row")
    return row // 2, row % 2, lax.axis_index("col")


def aligned(i):
    return pl.ds(pl.multiple_of(i * BLK, BLK), BLK)


def tile_mask(flag, a, p):
    rows = lax.broadcasted_iota(jnp.int32, (BLK, BLK), 0) < RANK
    cols = lax.broadcasted_iota(jnp.int32, (BLK, BLK), 1) < RANK
    f = [[flag(2 * a + i, 2 * p + j) for j in (0, 1)] for i in (0, 1)]
    return jnp.where(rows, jnp.where(cols, f[0][0], f[0][1]), jnp.where(cols, f[1][0], f[1][1])).astype(F32)


def masked_tile(flag, coupling, a, p):
    tile = coupling[aligned(a), aligned(p)] * tile_mask(flag, a, p).astype(BF16)
    return tile.T


def head_kernel(flags, coupling, left, right, cot, fin, own, packed, inputs, mine_far, mine, send, back_mask, *here):
    flags_s, coupling_s, left_s, right_s, cot_s, fin_s, sems = here
    rows = CLUS_DEV * CL // CHUNKS
    cases = cot.shape[1]
    pairs = [(flags, flags_s), (coupling, coupling_s), (left, left_s)]
    pairs += [(cot.at[pl.ds(i * rows, rows)], cot_s.at[pl.ds(i * rows, rows)]) for i in range(CHUNKS)]
    pairs += [(right, right_s)]
    pairs += [(fin.at[pl.ds(i * rows, rows)], fin_s.at[pl.ds(i * rows, rows)]) for i in range(CHUNKS)]
    copies = [pltpu.make_async_copy(src, dst, sems.at[i]) for i, (src, dst) in enumerate(pairs)]
    for copy in copies:
        copy.start()
    z, y, h = place()
    flag = lambda i, j: flags_s[i, 0, j]

    def project(at, basis, x, results):
        copies[at].wait()
        for c in range(CLUS_DEV):
            total = None
            for i in range(c * CHUNKS // CLUS_DEV, (c + 1) * CHUNKS // CLUS_DEV):
                copies[at + 1 + i].wait()
                part = slice(i * rows, (i + 1) * rows)
                term = dot(basis[:, part], x[part], NN)
                total = term if total is None else total + term
            for result in results:
                result[c * RANK : (c + 1) * RANK, :cases] = total.astype(BF16)

    copies[0].wait()
    copies[1].wait()
    for half in (0, 1):
        a = h if half == 0 else 1 - h
        for n in (0, 1):
            for ref, first, side in ((mine_far, 0, y), (packed, cases, 1 - y)):
                first += (2 * n + half) * BLK
                ref[:, first : first + BLK] = masked_tile(flag, coupling_s, a, 2 * (z ^ (3 - n)) + side)
    project(2, left_s, cot_s, (own, packed))
    for half in (0, 1):
        a = h if half == 0 else 1 - h
        cols = slice(half * BLK, (half + 1) * BLK)
        for k in (0, 1):
            at = slice(k * BLK, (k + 1) * BLK), cols
            mine[at] = masked_tile(flag, coupling_s, a, 2 * (z ^ k) + y)
            send[at] = masked_tile(flag, coupling_s, a, 2 * (z ^ k) + 1 - y)
        for k in range(4):
            back_mask[cols, k * BLK : (k + 1) * BLK] = tile_mask(flag, a, 2 * (z ^ k) + 1 - y).astype(BF16)
    project(3 + CHUNKS, right_s, fin_s, (inputs,))


def head(flags, coupling, left, right, cot, fin):
    cases = cot.shape[1]
    args = (flags, coupling, left, right, cot, fin)
    shapes = [(BLK, cases), (BLK, cases + 4 * BLK), (BLK, cases), (BLK, 4 * BLK)]
    shapes += [(2 * BLK, 2 * BLK)] * 2 + [(2 * BLK, 4 * BLK)]
    return call(
        head_kernel,
        [pltpu.VMEM(shape, BF16) for shape in shapes],
        *args,
        near=(pltpu.HBM,) * 6,
        scratch_shapes=[pltpu.SMEM(flags.shape, jnp.int32)]
        + [pltpu.VMEM(x.shape, BF16) for x in args[1:]]
        + [pltpu.SemaphoreType.DMA((4 + 2 * CHUNKS,))],
        name="head",
    )


def local_sum(mine, part, blocks):
    cases = blocks[0].shape[1]
    total = dot(mine[:, :BLK], blocks[0][...], NN) + dot(mine[:, BLK:], blocks[1][...], NN)
    return total + dot(part[:, :BLK], blocks[2][:, :cases], NN) + dot(part[:, BLK:], blocks[3][...], NN)


def far_kernel(n, got, mine, b0, b1, b2, b3, *refs):
    cols = slice(2 * n * BLK, 2 * (n + 1) * BLK)
    total = local_sum(mine[:, cols], b2[:, b0.shape[1] :][:, cols], (b0, b1, b2, b3))
    for ref in refs[:got]:
        total = total + ref[...].astype(F32)
    refs[-1][...] = total.astype(BF16)


def far_sum(n, mine, blocks, got=(), after=()):
    shape = pltpu.VMEM(blocks[0].shape, BF16)
    return call(functools.partial(far_kernel, n, len(got)), [shape], mine, *blocks, *got, *after, name="far")[0]


def near_sum_kernel(mine, part, b0, b1, b2, b3, *refs):
    out = refs[-1]
    out[...] = local_sum(mine[BLK:], part[BLK:], (b0, b1, b2, b3)).astype(BF16)


def near_sum(mine, part, blocks, after=()):
    return call(near_sum_kernel, [pltpu.VMEM(blocks[0].shape, BF16)], mine, part, *blocks, *after, name="near")[0]


def results_kernel(right, mine, part, b0, b1, b2, b3, s2, s3, own, back, last, back_mask, adjoint, grad, made, placed, sems):
    total = local_sum(mine[:BLK], part[:BLK], (b0, b1, b2, b3))
    total = total + s2[...].astype(F32) + s3[...].astype(F32)
    coupled = total.astype(BF16)
    rows = CLUS_DEV * CL // PIECES
    copies = []
    for i in range(PIECES):
        piece = pl.ds(i * rows, rows)
        c = i * rows // CL
        made[piece] = dot(right[:, i * rows : (i + 1) * rows], coupled[c * RANK : (c + 1) * RANK], TN).astype(BF16)
        copies.append(pltpu.make_async_copy(made.at[piece], adjoint.at[piece], sems.at[i]))
        copies[-1].start()
    z, y, h = place()
    for half in (0, 1):
        a = h if half == 0 else 1 - h
        for k in range(4):
            at = slice(half * BLK, (half + 1) * BLK), slice(k * BLK, (k + 1) * BLK)
            placed[aligned(a), aligned(2 * (z ^ k) + y)] = own[at]
            placed[aligned(a), aligned(2 * (z ^ k) + 1 - y)] = (back[at] if k < 3 else last[at[0], :]) * back_mask[at]
    copies.append(pltpu.make_async_copy(placed, grad, sems.at[PIECES]))
    copies[-1].start()
    for copy in copies:
        copy.wait()


def results(right_t, mine, part, blocks, *rest):
    shapes = [(CLUS_DEV * CL, blocks[0].shape[1]), (2 * BLK, 8 * BLK)]
    return call(
        results_kernel,
        [pltpu.HBM(shape, BF16) for shape in shapes],
        right_t,
        mine,
        part,
        *blocks,
        *rest,
        out_specs=(pl.BlockSpec(memory_space=pltpu.HBM),) * 2,
        scratch_shapes=[pltpu.VMEM(shape, BF16) for shape in shapes] + [pltpu.SemaphoreType.DMA((PIECES + 1,))],
        name="results",
    )


def tiles_kernel(after, b0, b1, *refs):
    out = refs[-1]
    for k, block in enumerate(refs[:-1]):
        cases = block.shape[1]
        cols = slice(k * BLK, (k + 1) * BLK)
        out[:BLK, cols] = dot(b0[:, :cases], block[...], NT).astype(BF16)
        out[BLK:, cols] = dot(b1[:, :cases], block[...], NT).astype(BF16)


def tiles(after, b0, b1, inputs, name):
    shape = pltpu.VMEM((2 * BLK, len(inputs) * BLK), BF16)
    return call(tiles_kernel, [shape], after, b0, b1, *inputs, name=name)[0]


def own_tiles_kernel(flags, *refs):
    z, y, h = place()
    tiles_kernel(*refs)
    out = refs[-1]
    for half in (0, 1):
        a = h if half == 0 else 1 - h
        for k in range(4):
            at = slice(half * BLK, (half + 1) * BLK), slice(k * BLK, (k + 1) * BLK)
            out[at] = out[at] * tile_mask(lambda i, j: flags[i, j], a, 2 * (z ^ k) + y).astype(BF16)


def own_tiles(flags, after, b0, b1, inputs):
    shape = pltpu.VMEM((2 * BLK, len(inputs) * BLK), BF16)
    return call(own_tiles_kernel, [shape], flags, after, b0, b1, *inputs, near=(pltpu.SMEM,), name="own_tiles")[0]


def swap_rows(x, bits):
    return lax.ppermute(x, "row", [(r, r ^ bits) for r in range(8)])


def swap_col(x):
    return lax.ppermute(x, "col", [(0, 1), (1, 0)])


def swap_both(x):
    return lax.ppermute(x, ("row", "col"), [(d, d ^ 3) for d in range(16)])


def together(*arrays):
    return lax.optimization_barrier(arrays)


def eight_rows(cotangent, forward_input, basis_left, basis_right, coupling, admissible):
    flags = admissible[:, 0, :]
    right_t = basis_right.T

    own, packed, inputs, mine_far, mine, send, back_mask = head(
        admissible, coupling[:, 0, :], basis_left.T, right_t, cotangent, forward_input
    )
    pair = swap_rows(packed, 1)
    pair_other = swap_both(own)
    other = swap_col(own)
    i1 = swap_rows(inputs, 2)
    i2 = swap_rows(inputs, 4)
    blocks = (own, other, pair, pair_other)
    l3 = far_sum(0, mine_far, blocks, (), (i1, i2))
    s1 = swap_rows(l3, 2)
    i3 = swap_rows(i2, 2)
    part = swap_rows(send, 1)
    l1 = near_sum(mine, part, blocks, ())
    s3 = swap_rows(l1, 2)
    l2 = far_sum(1, mine_far, blocks, (s1,), (l1,))
    s2 = swap_rows(l2, 4)
    back = swap_rows(tiles(l3, pair, pair_other, (inputs, i1, i2), "back3"), 1)
    last = swap_rows(tiles(l2, pair, pair_other, (i3,), "back1"), 1)
    tiles_here = own_tiles(flags, l3, own, other, (inputs, i1, i2, i3))
    adjoint, grad = results(right_t, mine, part, blocks, s2, s3, tiles_here, back, last, back_mask)
    return (adjoint, grad[:, None, :])


def project_any(basis, x):
    out = jnp.einsum(
        "cnr,cnk->crk",
        basis.reshape(CLUS_DEV, CL, RANK),
        x.reshape(CLUS_DEV, CL, -1),
        preferred_element_type=F32,
    )
    return out.astype(BF16).reshape(BLK, -1)


def any_rows(cotangent, forward_input, basis_left, basis_right, coupling, admissible):
    gathered = lax.all_gather(project_any(basis_left, cotangent), "col", axis=0, tiled=True)
    flags = admissible[:, 0, :].astype(BF16)
    widened = jnp.repeat(jnp.repeat(flags, RANK, axis=0), RANK, axis=1)
    masked = coupling[:, 0, :] * widened
    owned_columns = lax.all_to_all(masked, "row", split_axis=1, concat_axis=0, tiled=True)
    coupled = dot(owned_columns, lax.all_gather(gathered, "row", axis=0, tiled=True), TN).astype(BF16)
    adjoint = jnp.einsum(
        "cnr,crk->cnk",
        basis_right.reshape(CLUS_DEV, CL, RANK),
        coupled.reshape(CLUS_DEV, RANK, -1),
        preferred_element_type=F32,
    )
    adjoint = adjoint.astype(BF16).reshape(CLUS_DEV * CL, -1)
    inputs = project_any(basis_right, forward_input)
    outer = dot(gathered, lax.all_gather(inputs, "row", axis=0, tiled=True), NT)
    grad = (outer * widened.astype(F32)).astype(BF16)
    return (adjoint, grad[:, None, :])


def solution(mesh):
    return jax.shard_map(
        eight_rows if mesh.shape["row"] == 8 else any_rows,
        mesh=mesh,
        in_specs=(
            P(("row", "col"), "groups"),
            P(("row", "col"), "groups"),
            P(("row", "col"), None),
            P(("row", "col"), None),
            P("row", "col", None),
            P("row", "col", None),
        ),
        out_specs=(P(("row", "col"), "groups"), P(("groups", "row"), "col", None)),
        check_vma=False,
    )
```

```python
import functools

import jax
import jax.numpy as jnp
from jax import lax
from jax.experimental import pallas as pl
from jax.experimental.pallas import tpu as pltpu
from jax.sharding import PartitionSpec as P

CL = 1024
RANK = 64
CLUS_DEV = 2
BLK = CLUS_DEV * RANK
BF16 = jnp.bfloat16
F32 = jnp.float32

NN = (((1,), (0,)), ((), ()))
NT = (((1,), (1,)), ((), ()))
TN = (((0,), (0,)), ((), ()))
ROOM = 12 << 20
COST = {'zero': 0.1, 'head': 3, 'near': 0.3, 'far': 0.3, 'back': 0.3, 'back3': 0.3, 'back1': 0.3, 'own_tiles': 0.1, 'results': 4}
CHUNKS = 4
PIECES = 8


def dot(a, b, dims):
    return lax.dot_general(a, b, dims, preferred_element_type=F32)


def call(kernel, shapes, *args, near=(), name, **more):
    specs = [pl.BlockSpec(memory_space=m) for m in near]
    specs += [pl.BlockSpec(memory_space=pltpu.VMEM)] * (len(args) - len(near))
    held = [
        pltpu.with_memory_space_constraint(x, s.memory_space) if s.memory_space != pltpu.SMEM else x
        for s, x in zip(specs, args)
    ]
    more.setdefault("out_specs", tuple(pl.BlockSpec(memory_space=pltpu.VMEM) for _ in shapes))
    return pl.pallas_call(
        kernel,
        out_shape=tuple(shapes),
        in_specs=specs,
        name=name,
        compiler_params=pltpu.CompilerParams(vmem_limit_bytes=ROOM),
        cost_estimate=pl.CostEstimate(flops=int(COST.get(name, 1) * 1e9), bytes_accessed=0, transcendentals=0),
        **more,
    )(*held)


def place():
    row = lax.axis_index("row")
    return row // 2, row % 2, lax.axis_index("col")


def aligned(i):
    return pl.ds(pl.multiple_of(i * BLK, BLK), BLK)


def tile_mask(flag, a, p):
    rows = lax.broadcasted_iota(jnp.int32, (BLK, BLK), 0) < RANK
    cols = lax.broadcasted_iota(jnp.int32, (BLK, BLK), 1) < RANK
    f = [[flag(2 * a + i, 2 * p + j) for j in (0, 1)] for i in (0, 1)]
    return jnp.where(rows, jnp.where(cols, f[0][0], f[0][1]), jnp.where(cols, f[1][0], f[1][1])).astype(F32)


def masked_tile(flag, coupling, a, p):
    tile = coupling[aligned(a), aligned(p)] * tile_mask(flag, a, p).astype(BF16)
    return tile.T


def head_kernel(flags, coupling, left, right, cot, fin, own, packed, inputs, mine_far, mine, send, back_mask, *here):
    flags_s, coupling_s, left_s, right_s, cot_s, fin_s, sems = here
    rows = CLUS_DEV * CL // CHUNKS
    cases = cot.shape[1]
    pairs = [(flags, flags_s), (coupling, coupling_s), (left, left_s)]
    pairs += [(cot.at[pl.ds(i * rows, rows)], cot_s.at[pl.ds(i * rows, rows)]) for i in range(CHUNKS)]
    pairs += [(right, right_s)]
    pairs += [(fin.at[pl.ds(i * rows, rows)], fin_s.at[pl.ds(i * rows, rows)]) for i in range(CHUNKS)]
    copies = [pltpu.make_async_copy(src, dst, sems.at[i]) for i, (src, dst) in enumerate(pairs)]
    for copy in copies:
        copy.start()
    z, y, h = place()
    flag = lambda i, j: flags_s[i, 0, j]

    def project(at, basis, x, results):
        copies[at].wait()
        for c in range(CLUS_DEV):
            total = None
            for i in range(c * CHUNKS // CLUS_DEV, (c + 1) * CHUNKS // CLUS_DEV):
                copies[at + 1 + i].wait()
                part = slice(i * rows, (i + 1) * rows)
                term = dot(basis[:, part], x[part], NN)
                total = term if total is None else total + term
            for result in results:
                result[c * RANK : (c + 1) * RANK, :cases] = total.astype(BF16)

    copies[0].wait()
    copies[1].wait()
    for half in (0, 1):
        a = h if half == 0 else 1 - h
        for n in (0, 1):
            for ref, first, side in ((mine_far, 0, y), (packed, cases, 1 - y)):
                first += (2 * n + half) * BLK
                ref[:, first : first + BLK] = masked_tile(flag, coupling_s, a, 2 * (z ^ (3 - n)) + side)
    for half in (0, 1):
        a = h if half == 0 else 1 - h
        cols = slice(half * BLK, (half + 1) * BLK)
        for k in (0, 1):
            at = slice(k * BLK, (k + 1) * BLK), cols
            mine[at] = masked_tile(flag, coupling_s, a, 2 * (z ^ k) + y)
            send[at] = masked_tile(flag, coupling_s, a, 2 * (z ^ k) + 1 - y)
        for k in range(4):
            back_mask[cols, k * BLK : (k + 1) * BLK] = tile_mask(flag, a, 2 * (z ^ k) + 1 - y).astype(BF16)
    project(2, left_s, cot_s, (own, packed))
    project(3 + CHUNKS, right_s, fin_s, (inputs,))


def head(flags, coupling, left, right, cot, fin):
    cases = cot.shape[1]
    args = (flags, coupling, left, right, cot, fin)
    shapes = [(BLK, cases), (BLK, cases + 4 * BLK), (BLK, cases), (BLK, 4 * BLK)]
    shapes += [(2 * BLK, 2 * BLK)] * 2 + [(2 * BLK, 4 * BLK)]
    return call(
        head_kernel,
        [pltpu.VMEM(shape, BF16) for shape in shapes],
        *args,
        near=(pltpu.HBM,) * 6,
        scratch_shapes=[pltpu.SMEM(flags.shape, jnp.int32)]
        + [pltpu.VMEM(x.shape, BF16) for x in args[1:]]
        + [pltpu.SemaphoreType.DMA((4 + 2 * CHUNKS,))],
        name="head",
    )


def local_sum(mine, part, blocks):
    cases = blocks[0].shape[1]
    total = dot(mine[:, :BLK], blocks[0][...], NN) + dot(mine[:, BLK:], blocks[1][...], NN)
    return total + dot(part[:, :BLK], blocks[2][:, :cases], NN) + dot(part[:, BLK:], blocks[3][...], NN)


def far_kernel(n, got, mine, b0, b1, b2, b3, *refs):
    cols = slice(2 * n * BLK, 2 * (n + 1) * BLK)
    total = local_sum(mine[:, cols], b2[:, b0.shape[1] :][:, cols], (b0, b1, b2, b3))
    for ref in refs[:got]:
        total = total + ref[...].astype(F32)
    refs[-1][...] = total.astype(BF16)


def far_sum(n, mine, blocks, got=(), after=()):
    shape = pltpu.VMEM(blocks[0].shape, BF16)
    return call(functools.partial(far_kernel, n, len(got)), [shape], mine, *blocks, *got, *after, name="far")[0]


def near_sum_kernel(mine, part, b0, b1, b2, b3, *refs):
    out = refs[-1]
    out[...] = local_sum(mine[BLK:], part[BLK:], (b0, b1, b2, b3)).astype(BF16)


def near_sum(mine, part, blocks, after=()):
    return call(near_sum_kernel, [pltpu.VMEM(blocks[0].shape, BF16)], mine, part, *blocks, *after, name="near")[0]


def zero_kernel(mine, part, b0, b1, b2, b3, *refs):
    refs[-1][...] = local_sum(mine[:BLK], part[:BLK], (b0, b1, b2, b3))


def zero_sum(mine, part, blocks, after):
    return call(zero_kernel, [pltpu.VMEM(blocks[0].shape, F32)], mine, part, *blocks, *after, name="zero")[0]


def results_kernel(right, total, s2, s3, own, back, last, back_mask, adjoint, grad, made, placed, sems):
    coupled = (total[...] + s2[...].astype(F32) + s3[...].astype(F32)).astype(BF16)
    rows = CLUS_DEV * CL // PIECES
    copies = []
    for i in range(PIECES):
        piece = pl.ds(i * rows, rows)
        c = i * rows // CL
        made[piece] = dot(right[:, i * rows : (i + 1) * rows], coupled[c * RANK : (c + 1) * RANK], TN).astype(BF16)
        copies.append(pltpu.make_async_copy(made.at[piece], adjoint.at[piece], sems.at[i]))
        copies[-1].start()
    z, y, h = place()
    for half in (0, 1):
        a = h if half == 0 else 1 - h
        for k in range(4):
            at = slice(half * BLK, (half + 1) * BLK), slice(k * BLK, (k + 1) * BLK)
            placed[aligned(a), aligned(2 * (z ^ k) + y)] = own[at]
            placed[aligned(a), aligned(2 * (z ^ k) + 1 - y)] = (back[at] if k < 3 else last[at[0], :]) * back_mask[at]
    copies.append(pltpu.make_async_copy(placed, grad, sems.at[PIECES]))
    copies[-1].start()
    for copy in copies:
        copy.wait()


def results(right_t, total, *rest):
    shapes = [(CLUS_DEV * CL, total.shape[1]), (2 * BLK, 8 * BLK)]
    return call(
        results_kernel,
        [pltpu.HBM(shape, BF16) for shape in shapes],
        right_t,
        total,
        *rest,
        out_specs=(pl.BlockSpec(memory_space=pltpu.HBM),) * 2,
        scratch_shapes=[pltpu.VMEM(shape, BF16) for shape in shapes] + [pltpu.SemaphoreType.DMA((PIECES + 1,))],
        name="results",
    )


def tiles_kernel(after, b0, b1, *refs):
    out = refs[-1]
    for k, block in enumerate(refs[:-1]):
        cases = block.shape[1]
        cols = slice(k * BLK, (k + 1) * BLK)
        out[:BLK, cols] = dot(b0[:, :cases], block[...], NT).astype(BF16)
        out[BLK:, cols] = dot(b1[:, :cases], block[...], NT).astype(BF16)


def tiles(after, b0, b1, inputs, name):
    shape = pltpu.VMEM((2 * BLK, len(inputs) * BLK), BF16)
    return call(tiles_kernel, [shape], after, b0, b1, *inputs, name=name)[0]


def own_tiles_kernel(flags, *refs):
    z, y, h = place()
    tiles_kernel(*refs)
    out = refs[-1]
    for half in (0, 1):
        a = h if half == 0 else 1 - h
        for k in range(4):
            at = slice(half * BLK, (half + 1) * BLK), slice(k * BLK, (k + 1) * BLK)
            out[at] = out[at] * tile_mask(lambda i, j: flags[i, j], a, 2 * (z ^ k) + y).astype(BF16)


def own_tiles(flags, after, b0, b1, inputs):
    shape = pltpu.VMEM((2 * BLK, len(inputs) * BLK), BF16)
    return call(own_tiles_kernel, [shape], flags, after, b0, b1, *inputs, near=(pltpu.SMEM,), name="own_tiles")[0]


def swap_rows(x, bits):
    return lax.ppermute(x, "row", [(r, r ^ bits) for r in range(8)])


def swap_col(x):
    return lax.ppermute(x, "col", [(0, 1), (1, 0)])


def swap_both(x):
    return lax.ppermute(x, ("row", "col"), [(d, d ^ 3) for d in range(16)])


def together(*arrays):
    return lax.optimization_barrier(arrays)


def eight_rows(cotangent, forward_input, basis_left, basis_right, coupling, admissible):
    flags = admissible[:, 0, :]
    right_t = basis_right.T

    own, packed, inputs, mine_far, mine, send, back_mask = head(
        admissible, coupling[:, 0, :], basis_left.T, right_t, cotangent, forward_input
    )
    pair = swap_rows(packed, 1)
    pair_other = swap_both(own)
    other = swap_col(own)
    i1 = swap_rows(inputs, 2)
    i2 = swap_rows(inputs, 4)
    blocks = (own, other, pair, pair_other)
    l3 = far_sum(0, mine_far, blocks, (), (i1, i2))
    s1 = swap_rows(l3, 2)
    i3 = swap_rows(i2, 2)
    part = swap_rows(send, 1)
    l1 = near_sum(mine, part, blocks, ())
    s3 = swap_rows(l1, 2)
    l2 = far_sum(1, mine_far, blocks, (s1,), (l1,))
    s2 = swap_rows(l2, 4)
    back = swap_rows(tiles(l3, pair, pair_other, (inputs, i1, i2), "back3"), 1)
    last = swap_rows(tiles(l2, pair, pair_other, (i3,), "back1"), 1)
    tiles_here = own_tiles(flags, l3, own, other, (inputs, i1, i2, i3))
    adjoint, grad = results(right_t, zero_sum(mine, part, blocks, (l2,)), s2, s3, tiles_here, back, last, back_mask)
    return (adjoint, grad[:, None, :])


def project_any(basis, x):
    out = jnp.einsum(
        "cnr,cnk->crk",
        basis.reshape(CLUS_DEV, CL, RANK),
        x.reshape(CLUS_DEV, CL, -1),
        preferred_element_type=F32,
    )
    return out.astype(BF16).reshape(BLK, -1)


def any_rows(cotangent, forward_input, basis_left, basis_right, coupling, admissible):
    gathered = lax.all_gather(project_any(basis_left, cotangent), "col", axis=0, tiled=True)
    flags = admissible[:, 0, :].astype(BF16)
    widened = jnp.repeat(jnp.repeat(flags, RANK, axis=0), RANK, axis=1)
    masked = coupling[:, 0, :] * widened
    owned_columns = lax.all_to_all(masked, "row", split_axis=1, concat_axis=0, tiled=True)
    coupled = dot(owned_columns, lax.all_gather(gathered, "row", axis=0, tiled=True), TN).astype(BF16)
    adjoint = jnp.einsum(
        "cnr,crk->cnk",
        basis_right.reshape(CLUS_DEV, CL, RANK),
        coupled.reshape(CLUS_DEV, RANK, -1),
        preferred_element_type=F32,
    )
    adjoint = adjoint.astype(BF16).reshape(CLUS_DEV * CL, -1)
    inputs = project_any(basis_right, forward_input)
    outer = dot(gathered, lax.all_gather(inputs, "row", axis=0, tiled=True), NT)
    grad = (outer * widened.astype(F32)).astype(BF16)
    return (adjoint, grad[:, None, :])


def solution(mesh):
    return jax.shard_map(
        eight_rows if mesh.shape["row"] == 8 else any_rows,
        mesh=mesh,
        in_specs=(
            P(("row", "col"), "groups"),
            P(("row", "col"), "groups"),
            P(("row", "col"), None),
            P(("row", "col"), None),
            P("row", "col", None),
            P("row", "col", None),
        ),
        out_specs=(P(("row", "col"), "groups"), P(("groups", "row"), "col", None)),
        check_vma=False,
    )
```

```python
import functools

import jax
import jax.numpy as jnp
from jax import lax
from jax.experimental import pallas as pl
from jax.experimental.pallas import tpu as pltpu
from jax.sharding import PartitionSpec as P

CL = 1024
RANK = 64
CLUS_DEV = 2
BLK = CLUS_DEV * RANK
BF16 = jnp.bfloat16
F32 = jnp.float32

NN = (((1,), (0,)), ((), ()))
NT = (((1,), (1,)), ((), ()))
TN = (((0,), (0,)), ((), ()))
ROOM = 12 << 20
COST = {'zero': 0.1, 'head': 3, 'near': 0.3, 'far': 0.3, 'back': 0.3, 'back3': 0.3, 'back1': 0.3, 'own_tiles': 0.1, 'results': 4}
CHUNKS = 4
PIECES = 16


def dot(a, b, dims):
    return lax.dot_general(a, b, dims, preferred_element_type=F32)


def call(kernel, shapes, *args, near=(), name, **more):
    specs = [pl.BlockSpec(memory_space=m) for m in near]
    specs += [pl.BlockSpec(memory_space=pltpu.VMEM)] * (len(args) - len(near))
    held = [
        pltpu.with_memory_space_constraint(x, s.memory_space) if s.memory_space != pltpu.SMEM else x
        for s, x in zip(specs, args)
    ]
    more.setdefault("out_specs", tuple(pl.BlockSpec(memory_space=pltpu.VMEM) for _ in shapes))
    return pl.pallas_call(
        kernel,
        out_shape=tuple(shapes),
        in_specs=specs,
        name=name,
        compiler_params=pltpu.CompilerParams(vmem_limit_bytes=ROOM),
        cost_estimate=pl.CostEstimate(flops=int(COST.get(name, 1) * 1e9), bytes_accessed=0, transcendentals=0),
        **more,
    )(*held)


def place():
    row = lax.axis_index("row")
    return row // 2, row % 2, lax.axis_index("col")


def aligned(i):
    return pl.ds(pl.multiple_of(i * BLK, BLK), BLK)


def tile_mask(flag, a, p):
    rows = lax.broadcasted_iota(jnp.int32, (BLK, BLK), 0) < RANK
    cols = lax.broadcasted_iota(jnp.int32, (BLK, BLK), 1) < RANK
    f = [[flag(2 * a + i, 2 * p + j) for j in (0, 1)] for i in (0, 1)]
    return jnp.where(rows, jnp.where(cols, f[0][0], f[0][1]), jnp.where(cols, f[1][0], f[1][1])).astype(F32)


def masked_tile(flag, coupling, a, p):
    tile = coupling[aligned(a), aligned(p)] * tile_mask(flag, a, p).astype(BF16)
    return tile.T


def head_kernel(flags, coupling, left, right, cot, fin, own, packed, inputs, mine_far, mine, send, back_mask, *here):
    flags_s, coupling_s, left_s, right_s, cot_s, fin_s, sems = here
    rows = CLUS_DEV * CL // CHUNKS
    cases = cot.shape[1]
    pairs = [(flags, flags_s), (coupling, coupling_s), (left, left_s)]
    pairs += [(cot.at[pl.ds(i * rows, rows)], cot_s.at[pl.ds(i * rows, rows)]) for i in range(CHUNKS)]
    pairs += [(right, right_s)]
    pairs += [(fin.at[pl.ds(i * rows, rows)], fin_s.at[pl.ds(i * rows, rows)]) for i in range(CHUNKS)]
    copies = [pltpu.make_async_copy(src, dst, sems.at[i]) for i, (src, dst) in enumerate(pairs)]
    for copy in copies:
        copy.start()
    z, y, h = place()
    flag = lambda i, j: flags_s[i, 0, j]

    def project(at, basis, x, results):
        copies[at].wait()
        for c in range(CLUS_DEV):
            total = None
            for i in range(c * CHUNKS // CLUS_DEV, (c + 1) * CHUNKS // CLUS_DEV):
                copies[at + 1 + i].wait()
                part = slice(i * rows, (i + 1) * rows)
                term = dot(basis[:, part], x[part], NN)
                total = term if total is None else total + term
            for result in results:
                result[c * RANK : (c + 1) * RANK, :cases] = total.astype(BF16)

    copies[0].wait()
    copies[1].wait()
    for half in (0, 1):
        a = h if half == 0 else 1 - h
        for n in (0, 1):
            for ref, first, side in ((mine_far, 0, y), (packed, cases, 1 - y)):
                first += (2 * n + half) * BLK
                ref[:, first : first + BLK] = masked_tile(flag, coupling_s, a, 2 * (z ^ (3 - n)) + side)
    for half in (0, 1):
        a = h if half == 0 else 1 - h
        cols = slice(half * BLK, (half + 1) * BLK)
        for k in (0, 1):
            at = slice(k * BLK, (k + 1) * BLK), cols
            mine[at] = masked_tile(flag, coupling_s, a, 2 * (z ^ k) + y)
            send[at] = masked_tile(flag, coupling_s, a, 2 * (z ^ k) + 1 - y)
        for k in range(4):
            back_mask[cols, k * BLK : (k + 1) * BLK] = tile_mask(flag, a, 2 * (z ^ k) + 1 - y).astype(BF16)
    project(2, left_s, cot_s, (own, packed))
    project(3 + CHUNKS, right_s, fin_s, (inputs,))


def head(flags, coupling, left, right, cot, fin):
    cases = cot.shape[1]
    args = (flags, coupling, left, right, cot, fin)
    shapes = [(BLK, cases), (BLK, cases + 4 * BLK), (BLK, cases), (BLK, 4 * BLK)]
    shapes += [(2 * BLK, 2 * BLK)] * 2 + [(2 * BLK, 4 * BLK)]
    return call(
        head_kernel,
        [pltpu.VMEM(shape, BF16) for shape in shapes],
        *args,
        near=(pltpu.HBM,) * 6,
        scratch_shapes=[pltpu.SMEM(flags.shape, jnp.int32)]
        + [pltpu.VMEM(x.shape, BF16) for x in args[1:]]
        + [pltpu.SemaphoreType.DMA((4 + 2 * CHUNKS,))],
        name="head",
    )


def local_sum(mine, part, blocks):
    cases = blocks[0].shape[1]
    total = dot(mine[:, :BLK], blocks[0][...], NN) + dot(mine[:, BLK:], blocks[1][...], NN)
    return total + dot(part[:, :BLK], blocks[2][:, :cases], NN) + dot(part[:, BLK:], blocks[3][...], NN)


def far_kernel(n, got, mine, b0, b1, b2, b3, *refs):
    cols = slice(2 * n * BLK, 2 * (n + 1) * BLK)
    total = local_sum(mine[:, cols], b2[:, b0.shape[1] :][:, cols], (b0, b1, b2, b3))
    for ref in refs[:got]:
        total = total + ref[...].astype(F32)
    refs[-1][...] = total.astype(BF16)


def far_sum(n, mine, blocks, got=(), after=()):
    shape = pltpu.VMEM(blocks[0].shape, BF16)
    return call(functools.partial(far_kernel, n, len(got)), [shape], mine, *blocks, *got, *after, name="far")[0]


def near_sum_kernel(mine, part, b0, b1, b2, b3, *refs):
    out = refs[-1]
    out[...] = local_sum(mine[BLK:], part[BLK:], (b0, b1, b2, b3)).astype(BF16)


def near_sum(mine, part, blocks, after=()):
    return call(near_sum_kernel, [pltpu.VMEM(blocks[0].shape, BF16)], mine, part, *blocks, *after, name="near")[0]


def zero_kernel(right, mine, part, b0, b1, b2, b3, *refs):
    refs[-1][...] = right[...].T
    refs[-2][...] = local_sum(mine[:BLK], part[:BLK], (b0, b1, b2, b3))


def zero_sum(right_t, mine, part, blocks, after):
    shapes = [pltpu.VMEM(blocks[0].shape, F32), pltpu.VMEM(right_t.shape[::-1], BF16)]
    return call(zero_kernel, shapes, right_t, mine, part, *blocks, *after, name="zero")


def results_kernel(right, total, s2, s3, own, back, last, back_mask, adjoint, grad, made, placed, sems):
    coupled = (total[...] + s2[...].astype(F32) + s3[...].astype(F32)).astype(BF16)
    rows = CLUS_DEV * CL // PIECES
    copies = []
    for i in range(PIECES):
        piece = pl.ds(i * rows, rows)
        c = i * rows // CL
        made[piece] = dot(right[piece], coupled[c * RANK : (c + 1) * RANK], NN).astype(BF16)
        copies.append(pltpu.make_async_copy(made.at[piece], adjoint.at[piece], sems.at[i]))
        copies[-1].start()
    z, y, h = place()
    for half in (0, 1):
        a = h if half == 0 else 1 - h
        for k in range(4):
            at = slice(half * BLK, (half + 1) * BLK), slice(k * BLK, (k + 1) * BLK)
            placed[aligned(a), aligned(2 * (z ^ k) + y)] = own[at]
            placed[aligned(a), aligned(2 * (z ^ k) + 1 - y)] = (back[at] if k < 3 else last[at[0], :]) * back_mask[at]
    copies.append(pltpu.make_async_copy(placed, grad, sems.at[PIECES]))
    copies[-1].start()
    for copy in copies:
        copy.wait()


def results(right, total, *rest):
    shapes = [(CLUS_DEV * CL, total.shape[1]), (2 * BLK, 8 * BLK)]
    return call(
        results_kernel,
        [pltpu.HBM(shape, BF16) for shape in shapes],
        right,
        total,
        *rest,
        out_specs=(pl.BlockSpec(memory_space=pltpu.HBM),) * 2,
        scratch_shapes=[pltpu.VMEM(shape, BF16) for shape in shapes] + [pltpu.SemaphoreType.DMA((PIECES + 1,))],
        name="results",
    )


def tiles_kernel(after, b0, b1, *refs):
    out = refs[-1]
    for k, block in enumerate(refs[:-1]):
        cases = block.shape[1]
        cols = slice(k * BLK, (k + 1) * BLK)
        out[:BLK, cols] = dot(b0[:, :cases], block[...], NT).astype(BF16)
        out[BLK:, cols] = dot(b1[:, :cases], block[...], NT).astype(BF16)


def tiles(after, b0, b1, inputs, name):
    shape = pltpu.VMEM((2 * BLK, len(inputs) * BLK), BF16)
    return call(tiles_kernel, [shape], after, b0, b1, *inputs, name=name)[0]


def own_tiles_kernel(flags, *refs):
    z, y, h = place()
    tiles_kernel(*refs)
    out = refs[-1]
    for half in (0, 1):
        a = h if half == 0 else 1 - h
        for k in range(4):
            at = slice(half * BLK, (half + 1) * BLK), slice(k * BLK, (k + 1) * BLK)
            out[at] = out[at] * tile_mask(lambda i, j: flags[i, j], a, 2 * (z ^ k) + y).astype(BF16)


def own_tiles(flags, after, b0, b1, inputs):
    shape = pltpu.VMEM((2 * BLK, len(inputs) * BLK), BF16)
    return call(own_tiles_kernel, [shape], flags, after, b0, b1, *inputs, near=(pltpu.SMEM,), name="own_tiles")[0]


def swap_rows(x, bits):
    return lax.ppermute(x, "row", [(r, r ^ bits) for r in range(8)])


def swap_col(x):
    return lax.ppermute(x, "col", [(0, 1), (1, 0)])


def swap_both(x):
    return lax.ppermute(x, ("row", "col"), [(d, d ^ 3) for d in range(16)])


def together(*arrays):
    return lax.optimization_barrier(arrays)


def eight_rows(cotangent, forward_input, basis_left, basis_right, coupling, admissible):
    flags = admissible[:, 0, :]
    right_t = basis_right.T

    own, packed, inputs, mine_far, mine, send, back_mask = head(
        admissible, coupling[:, 0, :], basis_left.T, right_t, cotangent, forward_input
    )
    pair = swap_rows(packed, 1)
    pair_other = swap_both(own)
    other = swap_col(own)
    i1 = swap_rows(inputs, 2)
    i2 = swap_rows(inputs, 4)
    blocks = (own, other, pair, pair_other)
    l3 = far_sum(0, mine_far, blocks, (), (i1, i2))
    s1 = swap_rows(l3, 2)
    i3 = swap_rows(i2, 2)
    part = swap_rows(send, 1)
    l1 = near_sum(mine, part, blocks, ())
    s3 = swap_rows(l1, 2)
    l2 = far_sum(1, mine_far, blocks, (s1,), (l1,))
    s2 = swap_rows(l2, 4)
    back = swap_rows(tiles(l3, pair, pair_other, (inputs, i1, i2), "back3"), 1)
    last = swap_rows(tiles(l2, pair, pair_other, (i3,), "back1"), 1)
    tiles_here = own_tiles(flags, l3, own, other, (inputs, i1, i2, i3))
    total, right = zero_sum(right_t, mine, part, blocks, (l2,))
    adjoint, grad = results(right, total, s2, s3, tiles_here, back, last, back_mask)
    return (adjoint, grad[:, None, :])


def project_any(basis, x):
    out = jnp.einsum(
        "cnr,cnk->crk",
        basis.reshape(CLUS_DEV, CL, RANK),
        x.reshape(CLUS_DEV, CL, -1),
        preferred_element_type=F32,
    )
    return out.astype(BF16).reshape(BLK, -1)


def any_rows(cotangent, forward_input, basis_left, basis_right, coupling, admissible):
    gathered = lax.all_gather(project_any(basis_left, cotangent), "col", axis=0, tiled=True)
    flags = admissible[:, 0, :].astype(BF16)
    widened = jnp.repeat(jnp.repeat(flags, RANK, axis=0), RANK, axis=1)
    masked = coupling[:, 0, :] * widened
    owned_columns = lax.all_to_all(masked, "row", split_axis=1, concat_axis=0, tiled=True)
    coupled = dot(owned_columns, lax.all_gather(gathered, "row", axis=0, tiled=True), TN).astype(BF16)
    adjoint = jnp.einsum(
        "cnr,crk->cnk",
        basis_right.reshape(CLUS_DEV, CL, RANK),
        coupled.reshape(CLUS_DEV, RANK, -1),
        preferred_element_type=F32,
    )
    adjoint = adjoint.astype(BF16).reshape(CLUS_DEV * CL, -1)
    inputs = project_any(basis_right, forward_input)
    outer = dot(gathered, lax.all_gather(inputs, "row", axis=0, tiled=True), NT)
    grad = (outer * widened.astype(F32)).astype(BF16)
    return (adjoint, grad[:, None, :])


def solution(mesh):
    return jax.shard_map(
        eight_rows if mesh.shape["row"] == 8 else any_rows,
        mesh=mesh,
        in_specs=(
            P(("row", "col"), "groups"),
            P(("row", "col"), "groups"),
            P(("row", "col"), None),
            P(("row", "col"), None),
            P("row", "col", None),
            P("row", "col", None),
        ),
        out_specs=(P(("row", "col"), "groups"), P(("groups", "row"), "col", None)),
        check_vma=False,
    )
```
